32 devices in a mesh: dp: 8 (over z, x), lon: 4 (over y, core).
Axes of the slice: x: 2, y: 2, z: 4, core: 2. Of those that a mesh axis runs over, the one named last changes fastest.
Arguments:
- fields: bfloat16 [8, 32, 48, 768], P('dp', 'lon'), may hold values from -6 to 6
- cotangent: bfloat16 [8, 32, 48, 768], P('dp', 'lon'), may hold values from -6 to 6
- first_weight: bfloat16 [2, 8, 96, 96], replicated, may hold values from -0.4375 to 0.4375
- second_weight: bfloat16 [2, 8, 96, 96], replicated, may hold values from -0.4375 to 0.4375
Outputs:
- layer_out: bfloat16 [8, 32, 48, 768], P('dp', 'lon')
- field_grad: bfloat16 [8, 32, 48, 768], P('dp', 'lon')
- first_grad: float32 [2, 8, 96, 96], replicated
- second_grad: float32 [2, 8, 96, 96], replicated
The draws below stay inside these ranges and needn't reach their ends.
All inputs are finite; a program needn't handle non-finite values.
Results may differ from the reference program's by a relative error of at most 0.015.
Values may be sent and summed in bfloat16 or wider, within the bound.
No kernel may reach another device: no remote copies, remote signals or barrier semaphores. Data moves between devices by JAX's collectives and lax.ppermute only.
A program may use at most 64 MiB of HBM per device.

```python
import math
import jax
import jax.numpy as jnp
from jax import lax

C = 768
NB = 8
CB = 96
W = 32
KM = 16
LAT = 48
SAMPLES = 8


def block_scale(key, shape, pieces, low, top_value):
    loudness, own = 1.0, jax.random.fold_in(key, 6)
    for position, parts in pieces:
        draws = jnp.exp(jax.random.uniform(jax.random.fold_in(own, position), (parts,), jnp.float32, low / len(pieces), top_value / len(pieces)))
        loudness = loudness * jnp.repeat(draws, shape[position] // parts).reshape([-1 if axis == position else 1 for axis in range(len(shape))])
    return loudness


def normal_values(stream_key, extent, scale, reach, split=(), held_as=jnp.bfloat16):
    entries = jax.random.normal(stream_key, extent, jnp.float32) * scale
    if len(split) > 0:
        entries = block_scale(stream_key, extent, split, -0.22, 0.18) * entries
    return jnp.clip(entries, min=-reach, max=reach).astype(held_as)


def setup_inputs(seed: int = 0) -> dict:
    key_list = jax.random.split(jax.random.key(seed), 5)
    fields = normal_values(key_list[0], (SAMPLES, W, LAT, C), 1.0, 6.0, ((0, 8), (1, 4)))
    cotangent = normal_values(key_list[1], (SAMPLES, W, LAT, C), 1.0, 6.0, ((0, 8), (1, 4)))
    first_weight = normal_values(key_list[2], (2, NB, CB, CB), (2 * CB) ** -0.5, 0.4375)
    second_weight = normal_values(key_list[3], (2, NB, CB, CB), (2 * CB) ** -0.5, 0.4375)
    return {"fields": fields, "cotangent": cotangent, "first_weight": first_weight, "second_weight": second_weight}


COEF = 0.7978845608028654
CUBIC = 0.044715

def gelu_value(inner):
    hyper = jnp.tanh(COEF * (inner + CUBIC * inner * inner * inner))
    return 0.5 * inner * (1.0 + hyper)

def gelu_slope(inner):
    hyper = jnp.tanh(COEF * (inner + CUBIC * inner * inner * inner))
    return 0.5 * (1.0 + hyper) + 0.5 * inner * (1.0 - hyper * hyper) * COEF * (1.0 + 3.0 * CUBIC * inner * inner)

def make_basis(length, count):
    cell_idx = jnp.arange(length, dtype=jnp.int32)
    mode_idx = jnp.arange(count, dtype=jnp.int32)
    product = cell_idx[:, None] * mode_idx[None, :] % length
    angle = product.astype(jnp.float32) * jnp.float32(2.0 * math.pi / length)
    return jnp.stack([jnp.cos(angle), -jnp.sin(angle)], axis=-1).astype(jnp.bfloat16)

def lat_mix(part, table):
    return jnp.einsum('khc,hj->kjc', part.astype(jnp.float32), table.astype(jnp.float32))

def lat_forward(spec, lat_basis, lat_scale):
    real_in = spec[:, 0]
    imag_in = spec[:, 1]
    cos_tab = lat_basis[:, :, 0]
    sin_tab = lat_basis[:, :, 1]
    out_r = lat_mix(real_in, cos_tab) - lat_mix(imag_in, sin_tab)
    out_i = lat_mix(imag_in, cos_tab) + lat_mix(real_in, sin_tab)
    return (jnp.stack([out_r, out_i], axis=1) * lat_scale).astype(jnp.bfloat16)

def lat_inverse(spec, lat_basis, lat_scale):
    real_in = spec[:, 0]
    imag_in = spec[:, 1]
    cos_tab = lat_basis[:, :, 0]
    sin_tab = lat_basis[:, :, 1]
    out_r = lat_mix(real_in, cos_tab) + lat_mix(imag_in, sin_tab)
    out_i = lat_mix(imag_in, cos_tab) - lat_mix(real_in, sin_tab)
    return (jnp.stack([out_r, out_i], axis=1) * lat_scale).astype(jnp.bfloat16)

def mat_mul(left, right):
    return jnp.einsum('mhbi,bij->mhbj', left.astype(jnp.float32), right.astype(jnp.float32))

def mat_adj(left, right):
    return jnp.einsum('mhbj,bij->mhbi', left.astype(jnp.float32), right.astype(jnp.float32))

def mat_outer(left, right):
    return jnp.einsum('mhbi,mhbj->bij', left.astype(jnp.float32), right.astype(jnp.float32))

def block_product(real_in, imag_in, weight):
    return (mat_mul(real_in, weight[0]) - mat_mul(imag_in, weight[1]), mat_mul(real_in, weight[1]) + mat_mul(imag_in, weight[0]))

def block_adjoint(real_in, imag_in, weight):
    return (mat_adj(real_in, weight[0]) + mat_adj(imag_in, weight[1]), mat_adj(imag_in, weight[0]) - mat_adj(real_in, weight[1]))

def block_outer(left_r, left_i, right_r, right_i):
    return jnp.stack([mat_outer(left_r, right_r) + mat_outer(left_i, right_i), mat_outer(left_r, right_i) - mat_outer(left_i, right_r)])

def one_sample(pair, first_weight, second_weight):
    field_rows, cot_rows = pair
    dft_basis = make_basis(W, KM).astype(jnp.float32)
    lat_basis = make_basis(LAT, LAT)
    norm_scale = 1.0 / math.sqrt(W)
    lat_scale = 1.0 / math.sqrt(LAT)
    mode_idx = jnp.arange(KM, dtype=jnp.int32)
    mode_weight = jnp.where(mode_idx == 0, 1.0, 2.0).astype(jnp.bfloat16)[:, None, None, None]
    lon_spec = (jnp.einsum('whc,wkp->kphc', field_rows.astype(jnp.float32), dft_basis) * norm_scale).astype(jnp.bfloat16)
    spectrum = lat_forward(lon_spec, lat_basis, lat_scale)
    spec_r = spectrum[:, 0].reshape(KM, LAT, NB, CB)
    spec_i = spectrum[:, 1].reshape(KM, LAT, NB, CB)
    inner_r, inner_i = block_product(spec_r, spec_i, first_weight)
    act_real = gelu_value(inner_r).astype(jnp.bfloat16)
    act_imag = gelu_value(inner_i).astype(jnp.bfloat16)
    out_r, out_i = block_product(act_real, act_imag, second_weight)
    mixed = jnp.stack([out_r.astype(jnp.bfloat16), out_i.astype(jnp.bfloat16)], axis=1).reshape(KM, 2, LAT, C) * mode_weight
    mixed_lon = lat_inverse(mixed, lat_basis, lat_scale)
    wave = (jnp.einsum('kphc,wkp->whc', mixed_lon.astype(jnp.float32), dft_basis) * norm_scale).astype(jnp.bfloat16)
    layer_out = (field_rows.astype(jnp.float32) + wave.astype(jnp.float32)).astype(jnp.bfloat16)
    dual_lon = (jnp.einsum('whc,wkp->kphc', cot_rows.astype(jnp.float32), dft_basis) * norm_scale).astype(jnp.bfloat16)
    dual = lat_forward(dual_lon, lat_basis, lat_scale) * mode_weight
    dual_r = dual[:, 0].reshape(KM, LAT, NB, CB)
    dual_i = dual[:, 1].reshape(KM, LAT, NB, CB)
    back_r, back_i = block_adjoint(dual_r, dual_i, second_weight)
    pre_r = (back_r * gelu_slope(inner_r)).astype(jnp.bfloat16)
    pre_i = (back_i * gelu_slope(inner_i)).astype(jnp.bfloat16)
    bspec_r, bspec_i = block_adjoint(pre_r, pre_i, first_weight)
    back_spec = jnp.stack([bspec_r.astype(jnp.bfloat16), bspec_i.astype(jnp.bfloat16)], axis=1).reshape(KM, 2, LAT, C)
    back_lon = lat_inverse(back_spec, lat_basis, lat_scale)
    pull = (jnp.einsum('kphc,wkp->whc', back_lon.astype(jnp.float32), dft_basis) * norm_scale).astype(jnp.bfloat16)
    field_grad = (cot_rows.astype(jnp.float32) + pull.astype(jnp.float32)).astype(jnp.bfloat16)
    second_term = block_outer(act_real, act_imag, dual_r, dual_i)
    first_term = block_outer(spec_r, spec_i, pre_r, pre_i)
    return (layer_out, field_grad, first_term, second_term)

def reference(fields, cotangent, first_weight, second_weight):

    def run_one(pair):
        return one_sample(pair, first_weight, second_weight)
    layer_out, field_grad, first_terms, second_terms = lax.map(run_one, (fields, cotangent))
    first_grad = lax.optimization_barrier(jnp.sum(first_terms, axis=0)) / SAMPLES
    second_grad = lax.optimization_barrier(jnp.sum(second_terms, axis=0)) / SAMPLES
    return (layer_out, field_grad, first_grad, second_grad)
```

```python
import functools
import math

import jax
import jax.numpy as jnp
import ml_dtypes
import numpy as np
from jax import lax
from jax.experimental import pallas as pl
from jax.experimental.pallas import tpu as pltpu
from jax.sharding import PartitionSpec as P

COEF = 0.7978845608028654
CUBIC = 0.044715


def gelu_value(inner):
    hyper = jnp.tanh(COEF * (inner + CUBIC * inner * inner * inner))
    return 0.5 * inner * (1.0 + hyper)


def gelu_slope(inner):
    hyper = jnp.tanh(COEF * (inner + CUBIC * inner * inner * inner))
    return 0.5 * (1.0 + hyper) + 0.5 * inner * (1.0 - hyper * hyper) * COEF * (
        1.0 + 3.0 * CUBIC * inner * inner
    )


def make_basis(length, count):
    cell_idx = jnp.arange(length, dtype=jnp.int32)
    mode_idx = jnp.arange(count, dtype=jnp.int32)
    product = cell_idx[:, None] * mode_idx[None, :] % length
    angle = product.astype(jnp.float32) * jnp.float32(2.0 * math.pi / length)
    return jnp.stack([jnp.cos(angle), -jnp.sin(angle)], axis=-1).astype(jnp.bfloat16)


def lat_apply(spec, table, lat_scale):
    return (
        jnp.einsum("kphc,phqj->kqjc", spec, table, preferred_element_type=jnp.float32) * lat_scale
    ).astype(jnp.bfloat16)


def forward_weight(weight):
    return jnp.stack([jnp.stack([weight[0], weight[1]]), jnp.stack([-weight[1], weight[0]])])


def adjoint_weight(weight):
    return jnp.stack([jnp.stack([weight[0], -weight[1]]), jnp.stack([weight[1], weight[0]])])


def block_product(spec, stacked):
    return jnp.einsum("kphbi,pqbij->kqhbj", spec, stacked, preferred_element_type=jnp.float32)


def block_adjoint(spec, stacked):
    return jnp.einsum("kphbj,pqbij->kqhbi", spec, stacked, preferred_element_type=jnp.float32)


def block_outer(left, right):
    pairs = jnp.einsum("kphbi,kqhbj->pqbij", left, right, preferred_element_type=jnp.float32)
    return jnp.stack([pairs[0, 0] + pairs[1, 1], pairs[0, 1] - pairs[1, 0]])


def on_device(fields, cotangent, first_weight, second_weight):
    cell_rows = fields[0]
    cot_rows = cotangent[0]
    lat_rows = cell_rows.shape[1]
    channels = cell_rows.shape[2]
    groups = first_weight.shape[1]
    group_width = first_weight.shape[2]
    lon_count = lax.axis_size("lon")
    total_cells = cell_rows.shape[0] * lon_count
    dft_basis = make_basis(total_cells, total_cells // 2)
    lat_basis = make_basis(lat_rows, lat_rows)
    cos_tab = lat_basis[:, :, 0]
    sin_tab = lat_basis[:, :, 1]
    lat_fwd_table = jnp.stack(
        [jnp.stack([cos_tab, sin_tab], axis=1), jnp.stack([-sin_tab, cos_tab], axis=1)], axis=0
    )
    lat_inv_table = jnp.stack(
        [jnp.stack([cos_tab.T, -sin_tab.T], axis=1), jnp.stack([sin_tab.T, cos_tab.T], axis=1)],
        axis=0,
    )
    norm_scale = 1.0 / math.sqrt(total_cells)
    lat_scale = 1.0 / math.sqrt(lat_rows)
    local_modes = cell_rows.shape[0] // 2
    mode_idx = lax.axis_index("lon") * local_modes + jnp.arange(local_modes, dtype=jnp.int32)
    mode_weight = jnp.where(mode_idx == 0, 1.0, 2.0).astype(jnp.bfloat16)[:, None, None, None]
    first_fwd = forward_weight(first_weight)
    second_fwd = forward_weight(second_weight)
    first_adj = adjoint_weight(first_weight)
    second_adj = adjoint_weight(second_weight)

    def local_dft(all_lines):
        return (
            jnp.einsum("whc,wkp->kphc", all_lines, dft_basis, preferred_element_type=jnp.float32)
            * norm_scale
        ).astype(jnp.bfloat16)

    def local_idft(all_modes):
        return (
            jnp.einsum("kphc,wkp->whc", all_modes, dft_basis, preferred_element_type=jnp.float32)
            * norm_scale
        ).astype(jnp.bfloat16)

    def lines_to_modes(all_lines):
        return lax.all_to_all(local_dft(all_lines), "lon", split_axis=0, concat_axis=3, tiled=True)

    def modes_to_lines(all_modes):
        return lax.all_to_all(local_idft(all_modes), "lon", split_axis=0, concat_axis=2, tiled=True)

    def to_spectrum(grid_rows):
        return lines_to_modes(
            lax.all_to_all(grid_rows, "lon", split_axis=2, concat_axis=0, tiled=True)
        )

    def to_cells(spec_rows):
        return modes_to_lines(
            lax.all_to_all(spec_rows, "lon", split_axis=3, concat_axis=0, tiled=True)
        )

    def split_groups(spec_rows):
        return spec_rows.reshape(local_modes, 2, lat_rows, groups, group_width)

    def join_groups(spec_rows):
        return spec_rows.astype(jnp.bfloat16).reshape(local_modes, 2, lat_rows, channels)

    lon_spec = to_spectrum(cell_rows)
    spectrum = split_groups(lat_apply(lon_spec, lat_fwd_table, lat_scale))
    inner = block_product(spectrum, first_fwd)
    act = gelu_value(inner).astype(jnp.bfloat16)
    mixed = join_groups(block_product(act, second_fwd)) * mode_weight
    mixed_lon = lat_apply(mixed, lat_inv_table, lat_scale)
    wave = to_cells(mixed_lon)
    dual_lon = to_spectrum(cot_rows)
    dual = split_groups(lat_apply(dual_lon, lat_fwd_table, lat_scale) * mode_weight)
    back = block_adjoint(dual, second_adj)
    pre = (back * gelu_slope(inner)).astype(jnp.bfloat16)
    back_spec = join_groups(block_adjoint(pre, first_adj))
    back_lon = lat_apply(back_spec, lat_inv_table, lat_scale)
    pull = to_cells(back_lon)
    layer_out = (cell_rows.astype(jnp.float32) + wave.astype(jnp.float32)).astype(jnp.bfloat16)
    field_grad = (cot_rows.astype(jnp.float32) + pull.astype(jnp.float32)).astype(jnp.bfloat16)
    sample_count = lax.axis_size("dp")
    second_term = block_outer(act, dual) / sample_count
    first_term = block_outer(spectrum, pre) / sample_count
    first_grad, second_grad = lax.psum((first_term, second_term), ("dp", "lon"))
    return (layer_out[None], field_grad[None], first_grad, second_grad)


BF = jnp.bfloat16
F32 = jnp.float32


def dft_tables(cells, lat_rows):
    half = cells // 2

    def basis(length, count):
        product = np.arange(length)[:, None] * np.arange(count)[None, :] % length
        angle = product.astype(np.float32) * np.float32(2.0 * math.pi / length)
        pair = np.stack([np.cos(angle), -np.sin(angle)], axis=-1).astype(np.float32)
        return pair.astype(ml_dtypes.bfloat16).astype(np.float64)

    lon = basis(cells, half)[:half]
    lat = basis(lat_rows, lat_rows)
    scale = 1.0 / math.sqrt(cells * lat_rows)
    real = np.einsum("wk,hj->kjwh", lon[..., 0], lat[..., 0]) - np.einsum(
        "wk,hj->kjwh", lon[..., 1], lat[..., 1]
    )
    imag = np.einsum("wk,hj->kjwh", lon[..., 1], lat[..., 0]) + np.einsum(
        "wk,hj->kjwh", lon[..., 0], lat[..., 1]
    )
    both = np.stack([real, imag]) * scale
    size = half * lat_rows
    tables = [both[:, p::2].reshape(size, size).astype(ml_dtypes.bfloat16) for p in (0, 1)]
    forward = np.stack(tables)
    inverse = np.stack([t.T for t in tables])
    return forward, np.ascontiguousarray(inverse)


def dot(left, right):
    return jnp.dot(left, right, preferred_element_type=F32)


def dot_rows(left, right):
    return lax.dot_general(left, right, (((0,), (0,)), ((), ())), preferred_element_type=F32)


def pack(rows):
    half = rows.shape[0] // 2
    tail = rows[:, 128:]
    return jnp.concatenate(
        [rows[:, :128], jnp.concatenate([tail[:half], tail[half:]], axis=1)], axis=0
    )


def unpack(packed):
    count = packed.shape[0] * 2 // 3
    tail = packed[count:]
    return jnp.concatenate(
        [packed[:count], jnp.concatenate([tail[:, :64], tail[:, 64:]], axis=0)], axis=1
    )


def pack_kernel(me_ref, grid_ref, *outs):
    me = me_ref[0]
    _, cells, lat_rows, channels = grid_ref.shape
    width = channels // 4
    for here in range(4):

        @pl.when(me == here)
        def _():
            rows = grid_ref[...].reshape(cells * lat_rows, channels)
            for slot in range(4):
                there = here ^ slot
                outs[slot][...] = pack(rows[:, there * width : (there + 1) * width])


def merge_kernel(me_ref, grid_ref, *refs):
    slots, out_ref = refs[:4], refs[4]
    me = me_ref[0]
    _, cells, lat_rows, channels = grid_ref.shape
    for here in range(4):

        @pl.when(me == here)
        def _():
            rows = jnp.concatenate([unpack(slots[here ^ s][...]) for s in range(4)], axis=1)
            total = grid_ref[...].astype(F32) + rows.astype(F32).reshape(grid_ref.shape)
            out_ref[...] = total.astype(BF)


def load_halves(me, slots, sums, diffs):
    core = me % 2
    sign = jnp.where(me < 2, 1.0, -1.0).astype(F32)
    for slot, spot in ((0, core), (1, 1 - core)):
        near = unpack(slots[slot][...]).astype(F32)
        far = unpack(slots[slot + 2][...]).astype(F32)
        sums[spot] = (near + far).astype(BF)
        diffs[spot] = (sign * (near - far)).astype(BF)


def store_halves(me, outs, even, odd, even_ref, odd_ref):
    core = me % 2
    sign = jnp.where(me < 2, 1.0, -1.0).astype(F32)
    even_ref[...] = even.reshape(even_ref.shape)
    odd_ref[...] = odd.reshape(odd_ref.shape)
    for slot, spot in ((0, core), (1, 1 - core)):
        near = even_ref[spot]
        far = sign * odd_ref[spot]
        outs[slot][...] = pack((near + far).astype(BF))
        outs[slot + 2][...] = pack((near - far).astype(BF))


def mode_factor(shape, parity, lat_rows):
    if parity == 1:
        return 2.0
    row = lax.broadcasted_iota(jnp.int32, shape, 0)
    return jnp.where(row < lat_rows, 1.0, 2.0).astype(F32)


def gelu_both(u):
    square = u * u
    hyper = jnp.tanh(COEF * (u + CUBIC * square * u))
    value = 0.5 * u * (1.0 + hyper)
    slope = 0.5 * (1.0 + hyper) + 0.5 * u * (1.0 - hyper * hyper) * COEF * (
        1.0 + 3.0 * CUBIC * square
    )
    return value, slope


def forward_kernel(lat_rows, me_ref, *refs):
    slots = refs[:4]
    fwd_ref, inv_ref, first_ref, second_ref = refs[4:8]
    outs = refs[8:12]
    spec_ref, act_ref, slope_ref = refs[12:15]
    sums, diffs, even_ref, odd_ref = refs[15:]
    me = me_ref[0]
    load_halves(me, slots, sums, diffs)
    results = []
    for parity, half in ((0, sums), (1, diffs)):
        cells = half[...].reshape(-1, half.shape[-1])
        spec = dot(fwd_ref[parity], cells).astype(BF)
        size = spec.shape[0] // 2
        real, imag = spec[:size], spec[size:]
        spec_ref[parity] = spec
        inner_r = dot(real, first_ref[0]) - dot(imag, first_ref[1])
        inner_i = dot(real, first_ref[1]) + dot(imag, first_ref[0])
        act_r, slope_r = gelu_both(inner_r)
        act_i, slope_i = gelu_both(inner_i)
        act_r, act_i = act_r.astype(BF), act_i.astype(BF)
        act_ref[parity, :size] = act_r
        act_ref[parity, size:] = act_i
        slope_ref[parity, :size] = slope_r
        slope_ref[parity, size:] = slope_i
        factor = mode_factor(inner_r.shape, parity, lat_rows)
        mixed_r = ((dot(act_r, second_ref[0]) - dot(act_i, second_ref[1])) * factor).astype(BF)
        mixed_i = ((dot(act_r, second_ref[1]) + dot(act_i, second_ref[0])) * factor).astype(BF)
        results.append(dot(inv_ref[parity], jnp.concatenate([mixed_r, mixed_i], axis=0)))
    store_halves(me, outs, *results, even_ref, odd_ref)


def fold_groups(full):
    size = full.shape[0] // 2
    lane = lax.broadcasted_iota(jnp.int32, (size, full.shape[1]), 1)
    return jnp.where(lane < size, full[:size], full[size:])


def backward_kernel(lat_rows, me_ref, *refs):
    slots = refs[:4]
    fwd_ref, second_ref, spec_ref, act_ref, slope_ref = refs[4:9]
    pre_ref, grad_ref = refs[9:11]
    sums, diffs = refs[11:]
    me = me_ref[0]
    load_halves(me, slots, sums, diffs)
    grads = [0.0] * 4
    for parity, half in ((0, sums), (1, diffs)):
        cells = half[...].reshape(-1, half.shape[-1])
        dual = dot(fwd_ref[parity], cells)
        size = dual.shape[0] // 2
        factor = mode_factor(dual[:size].shape, parity, lat_rows)
        dual_r, dual_i = (dual[:size] * factor).astype(BF), (dual[size:] * factor).astype(BF)
        back_r = dot(dual_r, second_ref[0]) + dot(dual_i, second_ref[1])
        back_i = dot(dual_i, second_ref[0]) - dot(dual_r, second_ref[1])
        pre_r = (back_r * slope_ref[parity, :size]).astype(BF)
        pre_i = (back_i * slope_ref[parity, size:]).astype(BF)
        pre_ref[parity, :size] = pre_r
        pre_ref[parity, size:] = pre_i
        for spot, left, right_r, right_i in (
            (0, spec_ref, pre_r, pre_i),
            (2, act_ref, dual_r, dual_i),
        ):
            left_r, left_i = left[parity, :size], left[parity, size:]
            grads[spot] += dot_rows(left_r, right_r) + dot_rows(left_i, right_i)
            grads[spot + 1] += dot_rows(left_r, right_i) - dot_rows(left_i, right_r)
    grad_ref[...] = pack(jnp.concatenate([fold_groups(g) for g in grads], axis=0).astype(BF))


def return_kernel(me_ref, pre_ref, inv_ref, first_ref, *refs):
    outs = refs[:4]
    even_ref, odd_ref = refs[4:]
    me = me_ref[0]
    results = []
    for parity in (0, 1):
        size = pre_ref.shape[1] // 2
        pre_r, pre_i = pre_ref[parity, :size], pre_ref[parity, size:]
        spec_r = (dot(pre_r, first_ref[0]) + dot(pre_i, first_ref[1])).astype(BF)
        spec_i = (dot(pre_i, first_ref[0]) - dot(pre_r, first_ref[1])).astype(BF)
        results.append(dot(inv_ref[parity], jnp.concatenate([spec_r, spec_i], axis=0)))
    store_halves(me, outs, *results, even_ref, odd_ref)


def spread_kernel(scale, me_ref, *refs):
    slots, outs = refs[:4], refs[4:]
    me = me_ref[0]
    width = outs[0].shape[-1]
    for here in range(4):

        @pl.when(me == here)
        def _():
            for source in range(4):
                rows = unpack(slots[here ^ source][...]).astype(F32) * scale
                for tensor in range(2):
                    for part in range(2):
                        start = (tensor * 2 + part) * width
                        block = rows[start : start + width]
                        outs[tensor][part, 2 * source] = block[:, :width]
                        outs[tensor][part, 2 * source + 1] = block[:, width:]


VMEM = pl.BlockSpec(memory_space=pltpu.VMEM)
SMEM = pl.BlockSpec(memory_space=pltpu.SMEM)


def call(kernel, outs, args, scratch=(), flops=0):
    return pl.pallas_call(
        kernel,
        out_shape=outs,
        in_specs=[SMEM] + [VMEM] * (len(args) - 1),
        out_specs=[VMEM] * len(outs),
        scratch_shapes=scratch,
        compiler_params=pltpu.CompilerParams(vmem_limit_bytes=48 * 2**20),
        cost_estimate=pl.CostEstimate(
            flops=flops,
            bytes_accessed=sum(a.size * a.dtype.itemsize for a in (*args, *outs)),
            transcendentals=0,
        ),
    )(*args)


def swap(value, axis, mask):
    size = lax.axis_size(axis)
    return lax.ppermute(value, axis, [(i, i ^ mask) for i in range(size)])


def block_diag(weight, width):
    return jnp.pad(weight[:, 0], ((0, 0), (0, width), (0, width))) + jnp.pad(
        weight[:, 1], ((0, 0), (width, 0), (width, 0))
    )


def by_groups(fields, cotangent, first_weight, second_weight):
    _, cells, lat_rows, channels = fields.shape
    groups, group_width = first_weight.shape[1], first_weight.shape[2]
    lon_count = lax.axis_size("lon")
    sample_count = lax.axis_size("dp")
    per_device = groups // lon_count
    width = per_device * group_width
    total_cells = cells * lon_count
    rows = cells * lat_rows
    half = 2 * rows
    me = lax.axis_index("lon")
    me_arr = me.astype(jnp.int32).reshape(1)
    forward, inverse = (jnp.asarray(t) for t in dft_tables(total_cells, lat_rows))
    packed = jax.ShapeDtypeStruct((rows * width // 128, 128), BF)

    def own(weight):
        return lax.dynamic_slice_in_dim(weight, me * per_device, per_device, axis=1)

    first_own, second_own = own(first_weight), own(second_weight)
    first_mat = block_diag(first_own, group_width)
    second_mat = block_diag(second_own, group_width)
    first_adj = block_diag(first_own.swapaxes(2, 3), group_width)
    second_adj = block_diag(second_own.swapaxes(2, 3), group_width)

    def trade(slots):
        return [slots[0]] + [swap(slots[m], "lon", m) for m in range(1, lon_count)]

    halves = [pltpu.VMEM((2, rows, width), BF)] * 2
    results = [pltpu.VMEM((2, rows, width), F32)] * 2
    table_flops = 2 * 2 * half * half * width
    block_flops = 2 * 4 * half * width * width

    sent_fields = call(pack_kernel, [packed] * 4, [me_arr, fields])
    sent_cots = call(pack_kernel, [packed] * 4, [me_arr, cotangent])
    field_slots = trade(sent_fields)
    cot_slots = trade(sent_cots)
    spec_shape = jax.ShapeDtypeStruct((2, half, width), BF)
    slope_shape = jax.ShapeDtypeStruct((2, half, width), F32)
    *wave, spec, act, slope = call(
        functools.partial(forward_kernel, lat_rows),
        [packed] * 4 + [spec_shape, spec_shape, slope_shape],
        [me_arr, *field_slots, forward, inverse, first_mat, second_mat],
        halves + results,
        2 * table_flops + 2 * block_flops,
    )
    wave_slots = trade(wave)
    pre, grad = call(
        functools.partial(backward_kernel, lat_rows),
        [spec_shape, packed],
        [me_arr, *cot_slots, forward, second_adj, spec, act, slope],
        halves,
        table_flops + 3 * block_flops,
    )
    pull = call(
        return_kernel,
        [packed] * 4,
        [me_arr, pre, inverse, first_adj],
        results,
        table_flops + block_flops,
    )
    pull_slots = trade(pull)
    mask = 1
    while mask < sample_count:
        other = swap(grad, "dp", mask)
        grad = (grad.astype(F32) + other.astype(F32)).astype(BF)
        mask *= 2
    beyond = swap(grad, "lon", 2)
    near = swap(grad, "lon", 1)
    corner = swap(beyond, "lon", 1)
    grid_shape = jax.ShapeDtypeStruct(fields.shape, BF)
    (layer_out,) = call(merge_kernel, [grid_shape], [me_arr, fields, *wave_slots])
    (field_grad,) = call(merge_kernel, [grid_shape], [me_arr, cotangent, *pull_slots])
    grad_shape = jax.ShapeDtypeStruct(first_weight.shape, F32)
    first_grad, second_grad = call(
        functools.partial(spread_kernel, 1.0 / sample_count),
        [grad_shape] * 2,
        [me_arr, grad, near, beyond, corner],
    )
    return layer_out, field_grad, first_grad, second_grad


def owns_groups(mesh, fields, first_weight):
    lon_count, sample_count = mesh.shape["lon"], mesh.shape["dp"]
    _, cells, lat_rows, _ = fields.shape
    return (
        lon_count == 4
        and sample_count & (sample_count - 1) == 0
        and fields.shape[0] == sample_count
        and first_weight.shape[1:] == (8, 96, 96)
        and lat_rows % 16 == 0
        and cells % 8 == 0
    )


def solution(mesh):
    placed = (P("dp", "lon", None, None), P("dp", "lon", None, None), P(), P())

    def run(fields, cotangent, first_weight, second_weight):
        body = by_groups if owns_groups(mesh, fields, first_weight) else on_device
        return jax.shard_map(
            body, mesh=mesh, in_specs=placed, out_specs=placed, check_vma=False
        )(fields, cotangent, first_weight, second_weight)

    return run
```

```python
import functools
import math

import jax
import jax.numpy as jnp
import ml_dtypes
import numpy as np
from jax import lax
from jax.experimental import pallas as pl
from jax.experimental.pallas import tpu as pltpu
from jax.sharding import PartitionSpec as P

COEF = 0.7978845608028654
CUBIC = 0.044715


def gelu_value(inner):
    hyper = jnp.tanh(COEF * (inner + CUBIC * inner * inner * inner))
    return 0.5 * inner * (1.0 + hyper)


def gelu_slope(inner):
    hyper = jnp.tanh(COEF * (inner + CUBIC * inner * inner * inner))
    return 0.5 * (1.0 + hyper) + 0.5 * inner * (1.0 - hyper * hyper) * COEF * (
        1.0 + 3.0 * CUBIC * inner * inner
    )


def make_basis(length, count):
    cell_idx = jnp.arange(length, dtype=jnp.int32)
    mode_idx = jnp.arange(count, dtype=jnp.int32)
    product = cell_idx[:, None] * mode_idx[None, :] % length
    angle = product.astype(jnp.float32) * jnp.float32(2.0 * math.pi / length)
    return jnp.stack([jnp.cos(angle), -jnp.sin(angle)], axis=-1).astype(jnp.bfloat16)


def lat_apply(spec, table, lat_scale):
    return (
        jnp.einsum("kphc,phqj->kqjc", spec, table, preferred_element_type=jnp.float32) * lat_scale
    ).astype(jnp.bfloat16)


def forward_weight(weight):
    return jnp.stack([jnp.stack([weight[0], weight[1]]), jnp.stack([-weight[1], weight[0]])])


def adjoint_weight(weight):
    return jnp.stack([jnp.stack([weight[0], -weight[1]]), jnp.stack([weight[1], weight[0]])])


def block_product(spec, stacked):
    return jnp.einsum("kphbi,pqbij->kqhbj", spec, stacked, preferred_element_type=jnp.float32)


def block_adjoint(spec, stacked):
    return jnp.einsum("kphbj,pqbij->kqhbi", spec, stacked, preferred_element_type=jnp.float32)


def block_outer(left, right):
    pairs = jnp.einsum("kphbi,kqhbj->pqbij", left, right, preferred_element_type=jnp.float32)
    return jnp.stack([pairs[0, 0] + pairs[1, 1], pairs[0, 1] - pairs[1, 0]])


def on_device(fields, cotangent, first_weight, second_weight):
    cell_rows = fields[0]
    cot_rows = cotangent[0]
    lat_rows = cell_rows.shape[1]
    channels = cell_rows.shape[2]
    groups = first_weight.shape[1]
    group_width = first_weight.shape[2]
    lon_count = lax.axis_size("lon")
    total_cells = cell_rows.shape[0] * lon_count
    dft_basis = make_basis(total_cells, total_cells // 2)
    lat_basis = make_basis(lat_rows, lat_rows)
    cos_tab = lat_basis[:, :, 0]
    sin_tab = lat_basis[:, :, 1]
    lat_fwd_table = jnp.stack(
        [jnp.stack([cos_tab, sin_tab], axis=1), jnp.stack([-sin_tab, cos_tab], axis=1)], axis=0
    )
    lat_inv_table = jnp.stack(
        [jnp.stack([cos_tab.T, -sin_tab.T], axis=1), jnp.stack([sin_tab.T, cos_tab.T], axis=1)],
        axis=0,
    )
    norm_scale = 1.0 / math.sqrt(total_cells)
    lat_scale = 1.0 / math.sqrt(lat_rows)
    local_modes = cell_rows.shape[0] // 2
    mode_idx = lax.axis_index("lon") * local_modes + jnp.arange(local_modes, dtype=jnp.int32)
    mode_weight = jnp.where(mode_idx == 0, 1.0, 2.0).astype(jnp.bfloat16)[:, None, None, None]
    first_fwd = forward_weight(first_weight)
    second_fwd = forward_weight(second_weight)
    first_adj = adjoint_weight(first_weight)
    second_adj = adjoint_weight(second_weight)

    def local_dft(all_lines):
        return (
            jnp.einsum("whc,wkp->kphc", all_lines, dft_basis, preferred_element_type=jnp.float32)
            * norm_scale
        ).astype(jnp.bfloat16)

    def local_idft(all_modes):
        return (
            jnp.einsum("kphc,wkp->whc", all_modes, dft_basis, preferred_element_type=jnp.float32)
            * norm_scale
        ).astype(jnp.bfloat16)

    def lines_to_modes(all_lines):
        return lax.all_to_all(local_dft(all_lines), "lon", split_axis=0, concat_axis=3, tiled=True)

    def modes_to_lines(all_modes):
        return lax.all_to_all(local_idft(all_modes), "lon", split_axis=0, concat_axis=2, tiled=True)

    def to_spectrum(grid_rows):
        return lines_to_modes(
            lax.all_to_all(grid_rows, "lon", split_axis=2, concat_axis=0, tiled=True)
        )

    def to_cells(spec_rows):
        return modes_to_lines(
            lax.all_to_all(spec_rows, "lon", split_axis=3, concat_axis=0, tiled=True)
        )

    def split_groups(spec_rows):
        return spec_rows.reshape(local_modes, 2, lat_rows, groups, group_width)

    def join_groups(spec_rows):
        return spec_rows.astype(jnp.bfloat16).reshape(local_modes, 2, lat_rows, channels)

    lon_spec = to_spectrum(cell_rows)
    spectrum = split_groups(lat_apply(lon_spec, lat_fwd_table, lat_scale))
    inner = block_product(spectrum, first_fwd)
    act = gelu_value(inner).astype(jnp.bfloat16)
    mixed = join_groups(block_product(act, second_fwd)) * mode_weight
    mixed_lon = lat_apply(mixed, lat_inv_table, lat_scale)
    wave = to_cells(mixed_lon)
    dual_lon = to_spectrum(cot_rows)
    dual = split_groups(lat_apply(dual_lon, lat_fwd_table, lat_scale) * mode_weight)
    back = block_adjoint(dual, second_adj)
    pre = (back * gelu_slope(inner)).astype(jnp.bfloat16)
    back_spec = join_groups(block_adjoint(pre, first_adj))
    back_lon = lat_apply(back_spec, lat_inv_table, lat_scale)
    pull = to_cells(back_lon)
    layer_out = (cell_rows.astype(jnp.float32) + wave.astype(jnp.float32)).astype(jnp.bfloat16)
    field_grad = (cot_rows.astype(jnp.float32) + pull.astype(jnp.float32)).astype(jnp.bfloat16)
    sample_count = lax.axis_size("dp")
    second_term = block_outer(act, dual) / sample_count
    first_term = block_outer(spectrum, pre) / sample_count
    first_grad, second_grad = lax.psum((first_term, second_term), ("dp", "lon"))
    return (layer_out[None], field_grad[None], first_grad, second_grad)


BF = jnp.bfloat16
F32 = jnp.float32


def dft_tables(cells, lat_rows):
    half = cells // 2

    def basis(length, count):
        product = np.arange(length)[:, None] * np.arange(count)[None, :] % length
        angle = product.astype(np.float32) * np.float32(2.0 * math.pi / length)
        pair = np.stack([np.cos(angle), -np.sin(angle)], axis=-1).astype(np.float32)
        return pair.astype(ml_dtypes.bfloat16).astype(np.float64)

    lon = basis(cells, half)[:half]
    lat = basis(lat_rows, lat_rows)
    scale = 1.0 / math.sqrt(cells * lat_rows)
    real = np.einsum("wk,hj->kjwh", lon[..., 0], lat[..., 0]) - np.einsum(
        "wk,hj->kjwh", lon[..., 1], lat[..., 1]
    )
    imag = np.einsum("wk,hj->kjwh", lon[..., 1], lat[..., 0]) + np.einsum(
        "wk,hj->kjwh", lon[..., 0], lat[..., 1]
    )
    both = np.stack([real, imag]) * scale
    size = half * lat_rows
    tables = [both[:, p::2].reshape(size, size).astype(ml_dtypes.bfloat16) for p in (0, 1)]
    forward = np.stack(tables)
    inverse = np.stack([t.T for t in tables])
    return forward, np.ascontiguousarray(inverse)


def dot(left, right):
    return jnp.dot(left, right, preferred_element_type=F32)


def swap_groups(value):
    width = value.shape[-1] // 2
    return jnp.concatenate([value[:, width:], value[:, :width]], axis=1)


def choose(first, second):
    lane = lax.broadcasted_iota(jnp.int32, first.shape, 1)
    return jnp.where(lane < first.shape[1] // 2, first, second)


def pack(rows):
    half = rows.shape[0] // 2
    tail = rows[:, 128:]
    return jnp.concatenate(
        [rows[:, :128], jnp.concatenate([tail[:half], tail[half:]], axis=1)], axis=0
    )


def unpack(packed):
    count = packed.shape[0] * 2 // 3
    tail = packed[count:]
    return jnp.concatenate(
        [packed[:count], jnp.concatenate([tail[:, :64], tail[:, 64:]], axis=0)], axis=1
    )


def pack_kernel(grid_ref, *outs):
    me = lax.axis_index("lon")
    _, cells, lat_rows, channels = grid_ref.shape
    width = channels // 4
    for here in range(4):

        @pl.when(me == here)
        def _():
            rows = grid_ref[...].reshape(cells * lat_rows, channels)
            for slot in range(4):
                there = here ^ slot
                outs[slot][...] = pack(rows[:, there * width : (there + 1) * width])


def weight_kernel(first_ref, second_ref, table_hbm, *refs):
    outs, table_ref, sems = refs[:4], refs[4], refs[5]
    tables = [
        pltpu.make_async_copy(table_hbm.at[p], table_ref.at[p], sems.at[p]) for p in range(2)
    ]
    for copy in tables:
        copy.start()
    for i, weight_ref in enumerate((first_ref, second_ref)):
        for group in range(2):
            real, imag = weight_ref[0, group], weight_ref[1, group]
            cross = imag if group == 0 else -imag
            matrix = jnp.concatenate(
                [
                    jnp.concatenate([real, cross], axis=1),
                    jnp.concatenate([-cross, real], axis=1),
                ],
                axis=0,
            )
            outs[2 * i][group] = matrix
            outs[2 * i + 1][group] = matrix.T
    for copy in tables:
        copy.wait()


def merge_kernel(grid_ref, *refs):
    slots, out_ref = refs[:4], refs[4]
    me = lax.axis_index("lon")
    _, cells, lat_rows, channels = grid_ref.shape
    for here in range(4):

        @pl.when(me == here)
        def _():
            rows = jnp.concatenate([unpack(slots[here ^ s][...]) for s in range(4)], axis=1)
            total = grid_ref[...].astype(F32) + rows.astype(F32).reshape(grid_ref.shape)
            out_ref[...] = total.astype(BF)


def load_halves(me, slots, sums, diffs):
    core = me % 2
    sign = jnp.where(me < 2, 1.0, -1.0).astype(F32)
    for slot, spot in ((0, core), (1, 1 - core)):
        near = slots[slot][...].astype(F32)
        far = slots[slot + 2][...].astype(F32)
        for both, packed in ((sums, near + far), (diffs, sign * (near - far))):
            rows = unpack(packed.astype(BF))
            both[0, spot] = rows
            both[1, spot] = swap_groups(rows)


def to_modes(table, cells):
    size = table.shape[0] // 2
    straight, crossed = (cells[i].reshape(-1, cells.shape[-1]) for i in range(2))
    real = dot(table[:size], straight)
    imag = dot(table[size:], crossed)
    return choose(real, imag), choose(imag, real)


def to_cells(table, first, second):
    return dot(table, jnp.concatenate([choose(first, second), swap_groups(choose(second, first))], axis=0))


def store_halves(me, outs, even, odd, even_ref, odd_ref):
    core = me % 2
    sign = jnp.where(me < 2, 1.0, -1.0).astype(F32)
    even_ref[...] = even.reshape(even_ref.shape)
    odd_ref[...] = odd.reshape(odd_ref.shape)
    for slot, spot in ((0, core), (1, 1 - core)):
        near = even_ref[spot]
        far = sign * odd_ref[spot]
        outs[slot][...] = pack((near + far).astype(BF))
        outs[slot + 2][...] = pack((near - far).astype(BF))


def mode_factor(shape, parity, lat_rows):
    if parity == 1:
        return 2.0
    row = lax.broadcasted_iota(jnp.int32, shape, 0)
    return jnp.where(row < lat_rows, 1.0, 2.0).astype(F32)


def gelu_both(u):
    square = u * u
    hyper = jnp.tanh(COEF * (u + CUBIC * square * u))
    value = 0.5 * u * (1.0 + hyper)
    slope = 0.5 * (1.0 + hyper) + 0.5 * u * (1.0 - hyper * hyper) * COEF * (
        1.0 + 3.0 * CUBIC * square
    )
    return value, slope


def inner_kernel(*refs):
    slots = refs[:4]
    fwd_ref, first_ref = refs[4:6]
    act_ref, slope_ref, spec_t, act_t = refs[6:10]
    sums, diffs = refs[10:]
    load_halves(lax.axis_index("lon"), slots, sums, diffs)
    for parity, half in ((0, sums), (1, diffs)):
        modes = to_modes(fwd_ref[parity], half)
        for group in range(2):
            spec = modes[group].astype(BF)
            act, slope = gelu_both(dot(spec, first_ref[group]))
            act = act.astype(BF)
            size = act.shape[0]
            act_ref[parity, group] = act
            slope_ref[parity, group] = slope
            spec_t[group, :, parity * size : (parity + 1) * size] = spec.T
            act_t[group, :, parity * size : (parity + 1) * size] = act.T


def wave_kernel(lat_rows, act_ref, inv_ref, second_ref, *refs):
    outs = refs[:4]
    even_ref, odd_ref = refs[4:]
    results = []
    for parity in (0, 1):
        factor = mode_factor(act_ref.shape[2:], parity, lat_rows)
        mixed = [
            (dot(act_ref[parity, g], second_ref[g]) * factor).astype(BF) for g in range(2)
        ]
        results.append(to_cells(inv_ref[parity], *mixed))
    store_halves(lax.axis_index("lon"), outs, *results, even_ref, odd_ref)


def weight_terms(full, group):
    size = full.shape[0] // 2
    upper, lower = full[:size], swap_groups(full[size:])
    return choose(upper + lower, upper - lower if group == 0 else lower - upper)


def backward_kernel(lat_rows, *refs):
    slots = refs[:4]
    fwd_ref, second_ref, slope_ref, spec_t, act_t = refs[4:9]
    pre_ref, keep_ref, send_ref = refs[9:12]
    sums, diffs, grad_ref = refs[12:]
    load_halves(lax.axis_index("lon"), slots, sums, diffs)
    terms = [[0.0, 0.0], [0.0, 0.0]]
    for parity, half in ((0, sums), (1, diffs)):
        modes = to_modes(fwd_ref[parity], half)
        factor = mode_factor(modes[0].shape, parity, lat_rows)
        size = modes[0].shape[0]
        span = slice(parity * size, (parity + 1) * size)
        for group in range(2):
            dual = (modes[group] * factor).astype(BF)
            pre = (dot(dual, second_ref[group]) * slope_ref[parity, group]).astype(BF)
            pre_ref[parity, group] = pre
            terms[0][group] += dot(spec_t[group, :, span], pre)
            terms[1][group] += dot(act_t[group, :, span], dual)
    whole = jnp.concatenate([weight_terms(terms[t][g], g) for t in range(2) for g in range(2)], axis=0)
    grad_ref[...] = pack(whole.astype(BF)).reshape(grad_ref.shape)
    side = lax.axis_index("dp") % 2
    keep_ref[...] = grad_ref[side]
    send_ref[...] = grad_ref[1 - side]


def return_kernel(pre_ref, inv_ref, first_ref, *refs):
    outs = refs[:4]
    even_ref, odd_ref = refs[4:]
    results = []
    for parity in (0, 1):
        spec = [dot(pre_ref[parity, g], first_ref[g]).astype(BF) for g in range(2)]
        results.append(to_cells(inv_ref[parity], *spec))
    store_halves(lax.axis_index("lon"), outs, *results, even_ref, odd_ref)


def spread_kernel(scale, *refs):
    pieces, outs, whole, held, sems = refs[:8], refs[8:10], refs[10], refs[11], refs[12]
    me, side = lax.axis_index("lon"), lax.axis_index("dp") % 2
    width = held.shape[-1]
    copies = []
    for slot in (0, 1, 2, 3):
        source = me ^ slot
        whole[side] = pieces[2 * slot][...]
        whole[1 - side] = pieces[2 * slot + 1][...]
        rows = unpack(whole[...].reshape(-1, whole.shape[-1])).astype(F32) * scale
        for tensor in range(2):
            for group in range(2):
                start = (tensor * 2 + group) * width
                block = rows[start : start + width]
                held[slot, tensor, 0, group] = block[:, :width]
                held[slot, tensor, 1, group] = block[:, width:]
            copy = pltpu.make_async_copy(
                held.at[slot, tensor],
                outs[tensor].at[:, pl.ds(2 * source, 2)],
                sems.at[slot, tensor],
            )
            copy.start()
            copies.append(copy)
    for copy in copies:
        copy.wait()


VMEM = pl.BlockSpec(memory_space=pltpu.VMEM)
HBM = pl.BlockSpec(memory_space=pltpu.HBM)


def call(kernel, outs, args, scratch=(), in_hbm=(), out_hbm=False, vmem_mib=20):
    return pl.pallas_call(
        kernel,
        out_shape=outs,
        in_specs=[HBM if i in in_hbm else VMEM for i in range(len(args))],
        out_specs=[HBM if out_hbm else VMEM] * len(outs),
        scratch_shapes=scratch,
        compiler_params=pltpu.CompilerParams(vmem_limit_bytes=vmem_mib * 2**20),
        cost_estimate=pl.CostEstimate(flops=1, bytes_accessed=1, transcendentals=0),
    )(*args)


def swap(value, axis, mask):
    size = lax.axis_size(axis)
    return lax.ppermute(value, axis, [(i, i ^ mask) for i in range(size)])


def flip_pairs(dp_count, lon_count, dp_mask, lon_mask):
    return [
        (d * lon_count + i, (d ^ dp_mask) * lon_count + (i ^ lon_mask))
        for d in range(dp_count)
        for i in range(lon_count)
    ]


def after(*values):
    return lax.optimization_barrier(values)


def added(left, right):
    return (left.astype(F32) + right.astype(F32)).astype(BF)


def by_groups(fields, cotangent, first_weight, second_weight):
    _, cells, lat_rows, channels = fields.shape
    groups, group_width = first_weight.shape[1], first_weight.shape[2]
    lon_count = lax.axis_size("lon")
    sample_count = lax.axis_size("dp")
    width = groups // lon_count * group_width
    total_cells = cells * lon_count
    rows = cells * lat_rows
    half = 2 * rows
    forward, inverse = (jnp.asarray(t) for t in dft_tables(total_cells, lat_rows))
    packed = jax.ShapeDtypeStruct((rows * width // 128, 128), BF)
    piece = jax.ShapeDtypeStruct((4 * group_width * width // 256, 128), BF)

    def trade(slots):
        across, corner, beside = (swap(slots[m], "lon", m) for m in (2, 3, 1))
        return [slots[0], beside, across, corner]

    def own(weight):
        return lax.dynamic_slice_in_dim(weight, lax.axis_index("lon") * 2, 2, axis=1)

    halves = [pltpu.VMEM((2, 2, rows, width), BF)] * 2
    results = [pltpu.VMEM((2, rows, width), F32)] * 2

    field_slots = trade(call(pack_kernel, [packed] * 4, [fields]))
    cot_slots = trade(call(pack_kernel, [packed] * 4, [cotangent]))
    matrix = jax.ShapeDtypeStruct((2, width, width), BF)
    table = jax.ShapeDtypeStruct(forward.shape, BF)
    first_mat, first_adj, second_mat, second_adj, forward = call(
        weight_kernel,
        [matrix] * 4 + [table],
        [own(first_weight), own(second_weight), forward],
        [pltpu.SemaphoreType.DMA((2,))],
        in_hbm=(2,),
        vmem_mib=48,
    )
    modes_shape = jax.ShapeDtypeStruct((2, 2, rows, width), BF)
    slope_shape = jax.ShapeDtypeStruct((2, 2, rows, width), F32)
    turned_shape = jax.ShapeDtypeStruct((2, width, half), BF)
    act, slope, spec_t, act_t = call(
        inner_kernel,
        [modes_shape, slope_shape, turned_shape, turned_shape],
        [*field_slots, forward, first_mat],
        halves,
    )
    wave = call(
        functools.partial(wave_kernel, lat_rows), [packed] * 4, [act, inverse, second_mat], results
    )
    wave_slots = trade(wave)
    cot_slots, wave = after(cot_slots, wave)
    pre, keep, send = call(
        functools.partial(backward_kernel, lat_rows),
        [modes_shape, piece, piece],
        [*cot_slots, forward, second_adj, slope, spec_t, act_t],
        halves + [pltpu.VMEM((2, *piece.shape), BF)],
    )
    other = swap(send, "dp", 1)
    pull = call(return_kernel, [packed] * 4, [pre, inverse, first_adj], results)
    other, pull, wave_slots = after(other, pull, wave_slots)
    pull_slots = trade(pull)
    grad = added(keep, other)
    grid_shape = jax.ShapeDtypeStruct(fields.shape, BF)
    (layer_out,) = call(merge_kernel, [grid_shape], [fields, *wave_slots])
    mask = 2
    while mask < sample_count:
        other = swap(grad, "dp", mask)
        if mask == 4:
            other, layer_out, pull_slots = after(other, layer_out, pull_slots)
        grad = added(grad, other)
        mask *= 2
    beside = swap(grad, "lon", 1)
    beside, pull_slots = after(beside, pull_slots)
    (field_grad,) = call(merge_kernel, [grid_shape], [cotangent, *pull_slots])
    pieces = []
    for lon_mask in (0, 2):
        for dp_mask in (0, 1):
            pairs = flip_pairs(sample_count, lon_count, dp_mask, lon_mask)
            pieces.append(lax.ppermute(grad, ("dp", "lon"), pairs) if dp_mask + lon_mask else grad)
    pieces[3], field_grad = after(pieces[3], field_grad)
    across = [beside] + [swap(p, "lon", 1) for p in pieces[1:]]
    ordered = pieces[:2] + across[:2] + pieces[2:] + across[2:]
    grad_shape = jax.ShapeDtypeStruct(first_weight.shape, F32)
    first_grad, second_grad = call(
        functools.partial(spread_kernel, 1.0 / sample_count),
        [grad_shape] * 2,
        ordered,
        [
            pltpu.VMEM((2, *piece.shape), BF),
            pltpu.VMEM((4, 2, 2, 2, group_width, group_width), F32),
            pltpu.SemaphoreType.DMA((4, 2)),
        ],
        out_hbm=True,
    )
    return layer_out, field_grad, first_grad, second_grad


def owns_groups(mesh, fields, first_weight):
    lon_count, sample_count = mesh.shape["lon"], mesh.shape["dp"]
    _, cells, lat_rows, _ = fields.shape
    return (
        lon_count == 4
        and sample_count > 1
        and sample_count & (sample_count - 1) == 0
        and fields.shape[0] == sample_count
        and first_weight.shape[1:] == (8, 96, 96)
        and lat_rows % 16 == 0
        and cells % 8 == 0
    )


def solution(mesh):
    placed = (P("dp", "lon", None, None), P("dp", "lon", None, None), P(), P())

    def run(fields, cotangent, first_weight, second_weight):
        body = by_groups if owns_groups(mesh, fields, first_weight) else on_device
        return jax.shard_map(
            body, mesh=mesh, in_specs=placed, out_specs=placed, check_vma=False
        )(fields, cotangent, first_weight, second_weight)

    return run
```

```python
import functools
import math

import jax
import jax.numpy as jnp
import ml_dtypes
import numpy as np
from jax import lax
from jax.experimental import pallas as pl
from jax.experimental.pallas import tpu as pltpu
from jax.sharding import PartitionSpec as P

COEF = 0.7978845608028654
CUBIC = 0.044715


def gelu_value(inner):
    hyper = jnp.tanh(COEF * (inner + CUBIC * inner * inner * inner))
    return 0.5 * inner * (1.0 + hyper)


def gelu_slope(inner):
    hyper = jnp.tanh(COEF * (inner + CUBIC * inner * inner * inner))
    return 0.5 * (1.0 + hyper) + 0.5 * inner * (1.0 - hyper * hyper) * COEF * (
        1.0 + 3.0 * CUBIC * inner * inner
    )


def make_basis(length, count):
    cell_idx = jnp.arange(length, dtype=jnp.int32)
    mode_idx = jnp.arange(count, dtype=jnp.int32)
    product = cell_idx[:, None] * mode_idx[None, :] % length
    angle = product.astype(jnp.float32) * jnp.float32(2.0 * math.pi / length)
    return jnp.stack([jnp.cos(angle), -jnp.sin(angle)], axis=-1).astype(jnp.bfloat16)


def lat_apply(spec, table, lat_scale):
    return (
        jnp.einsum("kphc,phqj->kqjc", spec, table, preferred_element_type=jnp.float32) * lat_scale
    ).astype(jnp.bfloat16)


def forward_weight(weight):
    return jnp.stack([jnp.stack([weight[0], weight[1]]), jnp.stack([-weight[1], weight[0]])])


def adjoint_weight(weight):
    return jnp.stack([jnp.stack([weight[0], -weight[1]]), jnp.stack([weight[1], weight[0]])])


def block_product(spec, stacked):
    return jnp.einsum("kphbi,pqbij->kqhbj", spec, stacked, preferred_element_type=jnp.float32)


def block_adjoint(spec, stacked):
    return jnp.einsum("kphbj,pqbij->kqhbi", spec, stacked, preferred_element_type=jnp.float32)


def block_outer(left, right):
    pairs = jnp.einsum("kphbi,kqhbj->pqbij", left, right, preferred_element_type=jnp.float32)
    return jnp.stack([pairs[0, 0] + pairs[1, 1], pairs[0, 1] - pairs[1, 0]])


def on_device(fields, cotangent, first_weight, second_weight):
    cell_rows = fields[0]
    cot_rows = cotangent[0]
    lat_rows = cell_rows.shape[1]
    channels = cell_rows.shape[2]
    groups = first_weight.shape[1]
    group_width = first_weight.shape[2]
    lon_count = lax.axis_size("lon")
    total_cells = cell_rows.shape[0] * lon_count
    dft_basis = make_basis(total_cells, total_cells // 2)
    lat_basis = make_basis(lat_rows, lat_rows)
    cos_tab = lat_basis[:, :, 0]
    sin_tab = lat_basis[:, :, 1]
    lat_fwd_table = jnp.stack(
        [jnp.stack([cos_tab, sin_tab], axis=1), jnp.stack([-sin_tab, cos_tab], axis=1)], axis=0
    )
    lat_inv_table = jnp.stack(
        [jnp.stack([cos_tab.T, -sin_tab.T], axis=1), jnp.stack([sin_tab.T, cos_tab.T], axis=1)],
        axis=0,
    )
    norm_scale = 1.0 / math.sqrt(total_cells)
    lat_scale = 1.0 / math.sqrt(lat_rows)
    local_modes = cell_rows.shape[0] // 2
    mode_idx = lax.axis_index("lon") * local_modes + jnp.arange(local_modes, dtype=jnp.int32)
    mode_weight = jnp.where(mode_idx == 0, 1.0, 2.0).astype(jnp.bfloat16)[:, None, None, None]
    first_fwd = forward_weight(first_weight)
    second_fwd = forward_weight(second_weight)
    first_adj = adjoint_weight(first_weight)
    second_adj = adjoint_weight(second_weight)

    def local_dft(all_lines):
        return (
            jnp.einsum("whc,wkp->kphc", all_lines, dft_basis, preferred_element_type=jnp.float32)
            * norm_scale
        ).astype(jnp.bfloat16)

    def local_idft(all_modes):
        return (
            jnp.einsum("kphc,wkp->whc", all_modes, dft_basis, preferred_element_type=jnp.float32)
            * norm_scale
        ).astype(jnp.bfloat16)

    def lines_to_modes(all_lines):
        return lax.all_to_all(local_dft(all_lines), "lon", split_axis=0, concat_axis=3, tiled=True)

    def modes_to_lines(all_modes):
        return lax.all_to_all(local_idft(all_modes), "lon", split_axis=0, concat_axis=2, tiled=True)

    def to_spectrum(grid_rows):
        return lines_to_modes(
            lax.all_to_all(grid_rows, "lon", split_axis=2, concat_axis=0, tiled=True)
        )

    def to_cells(spec_rows):
        return modes_to_lines(
            lax.all_to_all(spec_rows, "lon", split_axis=3, concat_axis=0, tiled=True)
        )

    def split_groups(spec_rows):
        return spec_rows.reshape(local_modes, 2, lat_rows, groups, group_width)

    def join_groups(spec_rows):
        return spec_rows.astype(jnp.bfloat16).reshape(local_modes, 2, lat_rows, channels)

    lon_spec = to_spectrum(cell_rows)
    spectrum = split_groups(lat_apply(lon_spec, lat_fwd_table, lat_scale))
    inner = block_product(spectrum, first_fwd)
    act = gelu_value(inner).astype(jnp.bfloat16)
    mixed = join_groups(block_product(act, second_fwd)) * mode_weight
    mixed_lon = lat_apply(mixed, lat_inv_table, lat_scale)
    wave = to_cells(mixed_lon)
    dual_lon = to_spectrum(cot_rows)
    dual = split_groups(lat_apply(dual_lon, lat_fwd_table, lat_scale) * mode_weight)
    back = block_adjoint(dual, second_adj)
    pre = (back * gelu_slope(inner)).astype(jnp.bfloat16)
    back_spec = join_groups(block_adjoint(pre, first_adj))
    back_lon = lat_apply(back_spec, lat_inv_table, lat_scale)
    pull = to_cells(back_lon)
    layer_out = (cell_rows.astype(jnp.float32) + wave.astype(jnp.float32)).astype(jnp.bfloat16)
    field_grad = (cot_rows.astype(jnp.float32) + pull.astype(jnp.float32)).astype(jnp.bfloat16)
    sample_count = lax.axis_size("dp")
    second_term = block_outer(act, dual) / sample_count
    first_term = block_outer(spectrum, pre) / sample_count
    first_grad, second_grad = lax.psum((first_term, second_term), ("dp", "lon"))
    return (layer_out[None], field_grad[None], first_grad, second_grad)


BF = jnp.bfloat16
F32 = jnp.float32


def dft_tables(cells, lat_rows):
    half = cells // 2

    def basis(length, count):
        product = np.arange(length)[:, None] * np.arange(count)[None, :] % length
        angle = product.astype(np.float32) * np.float32(2.0 * math.pi / length)
        pair = np.stack([np.cos(angle), -np.sin(angle)], axis=-1).astype(np.float32)
        return pair.astype(ml_dtypes.bfloat16).astype(np.float64)

    lon = basis(cells, half)[:half]
    lat = basis(lat_rows, lat_rows)
    scale = 1.0 / math.sqrt(cells * lat_rows)
    real = np.einsum("wk,hj->kjwh", lon[..., 0], lat[..., 0]) - np.einsum(
        "wk,hj->kjwh", lon[..., 1], lat[..., 1]
    )
    imag = np.einsum("wk,hj->kjwh", lon[..., 1], lat[..., 0]) + np.einsum(
        "wk,hj->kjwh", lon[..., 0], lat[..., 1]
    )
    both = np.stack([real, imag]) * scale
    size = half * lat_rows
    tables = [both[:, p::2].reshape(size, size).astype(ml_dtypes.bfloat16) for p in (0, 1)]
    forward = np.stack(tables)
    inverse = np.stack([t.T for t in tables])
    return forward, np.ascontiguousarray(inverse)


def dot(left, right):
    return jnp.dot(left, right, preferred_element_type=F32)


def swap_groups(value):
    width = value.shape[-1] // 2
    return jnp.concatenate([value[:, width:], value[:, :width]], axis=1)


def choose(first, second):
    lane = lax.broadcasted_iota(jnp.int32, first.shape, 1)
    return jnp.where(lane < first.shape[1] // 2, first, second)


def pack(rows):
    half = rows.shape[0] // 2
    tail = rows[:, 128:]
    return jnp.concatenate(
        [rows[:, :128], jnp.concatenate([tail[:half], tail[half:]], axis=1)], axis=0
    )


def unpack(packed):
    count = packed.shape[0] * 2 // 3
    tail = packed[count:]
    return jnp.concatenate(
        [packed[:count], jnp.concatenate([tail[:, :64], tail[:, 64:]], axis=0)], axis=1
    )


def pack_kernel(grid_ref, *outs):
    me = lax.axis_index("lon")
    _, cells, lat_rows, channels = grid_ref.shape
    width = channels // 4
    for here in range(4):

        @pl.when(me == here)
        def _():
            rows = grid_ref[...].reshape(cells * lat_rows, channels)
            for slot in range(4):
                there = here ^ slot
                outs[slot][...] = pack(rows[:, there * width : (there + 1) * width])


def weight_kernel(first_ref, second_ref, table_hbm, *refs):
    outs, table_ref, sems = refs[:4], refs[4], refs[5]
    tables = [
        pltpu.make_async_copy(table_hbm.at[p], table_ref.at[p], sems.at[p]) for p in range(2)
    ]
    for copy in tables:
        copy.start()
    for i, weight_ref in enumerate((first_ref, second_ref)):
        for group in range(2):
            real, imag = weight_ref[0, group], weight_ref[1, group]
            cross = imag if group == 0 else -imag
            matrix = jnp.concatenate(
                [
                    jnp.concatenate([real, cross], axis=1),
                    jnp.concatenate([-cross, real], axis=1),
                ],
                axis=0,
            )
            outs[2 * i][group] = matrix
            outs[2 * i + 1][group] = matrix.T
    for copy in tables:
        copy.wait()


def merge_kernel(grid_ref, *refs):
    slots, out_ref = refs[:4], refs[4]
    me = lax.axis_index("lon")
    _, cells, lat_rows, channels = grid_ref.shape
    for here in range(4):

        @pl.when(me == here)
        def _():
            rows = jnp.concatenate([unpack(slots[here ^ s][...]) for s in range(4)], axis=1)
            total = grid_ref[...].astype(F32) + rows.astype(F32).reshape(grid_ref.shape)
            out_ref[...] = total.astype(BF)


def load_halves(me, slots, sums, diffs):
    core = me % 2
    sign = jnp.where(me < 2, 1.0, -1.0).astype(F32)
    for slot, spot in ((0, core), (1, 1 - core)):
        near = slots[slot][...].astype(F32)
        far = slots[slot + 2][...].astype(F32)
        for both, packed in ((sums, near + far), (diffs, sign * (near - far))):
            rows = unpack(packed.astype(BF))
            both[0, spot] = rows
            both[1, spot] = swap_groups(rows)


def to_modes(table, cells):
    size = table.shape[0] // 2
    straight, crossed = (cells[i].reshape(-1, cells.shape[-1]) for i in range(2))
    real = dot(table[:size], straight)
    imag = dot(table[size:], crossed)
    return choose(real, imag), choose(imag, real)


def to_cells(table, first, second):
    return dot(table, jnp.concatenate([choose(first, second), swap_groups(choose(second, first))], axis=0))


def store_halves(me, outs, even, odd, even_ref, odd_ref):
    core = me % 2
    sign = jnp.where(me < 2, 1.0, -1.0).astype(F32)
    even_ref[...] = even.reshape(even_ref.shape)
    odd_ref[...] = odd.reshape(odd_ref.shape)
    for slot, spot in ((0, core), (1, 1 - core)):
        near = even_ref[spot]
        far = sign * odd_ref[spot]
        outs[slot][...] = pack((near + far).astype(BF))
        outs[slot + 2][...] = pack((near - far).astype(BF))


def mode_factor(shape, parity, lat_rows):
    if parity == 1:
        return 2.0
    row = lax.broadcasted_iota(jnp.int32, shape, 0)
    return jnp.where(row < lat_rows, 1.0, 2.0).astype(F32)


def gelu_both(u):
    square = u * u
    hyper = jnp.tanh(COEF * (u + CUBIC * square * u))
    value = 0.5 * u * (1.0 + hyper)
    slope = 0.5 * (1.0 + hyper) + 0.5 * u * (1.0 - hyper * hyper) * COEF * (
        1.0 + 3.0 * CUBIC * square
    )
    return value, slope


def inner_kernel(*refs):
    slots = refs[:4]
    fwd_ref, first_ref = refs[4:6]
    act_ref, slope_ref, spec_t, act_t = refs[6:10]
    sums, diffs = refs[10:]
    load_halves(lax.axis_index("lon"), slots, sums, diffs)
    for parity, half in ((0, sums), (1, diffs)):
        modes = to_modes(fwd_ref[parity], half)
        for group in range(2):
            spec = modes[group].astype(BF)
            act, slope = gelu_both(dot(spec, first_ref[group]))
            act = act.astype(BF)
            size = act.shape[0]
            act_ref[parity, group] = act
            slope_ref[parity, group] = slope
            spec_t[group, :, parity * size : (parity + 1) * size] = spec.T
            act_t[group, :, parity * size : (parity + 1) * size] = act.T


def wave_kernel(lat_rows, act_ref, inv_ref, second_ref, *refs):
    outs = refs[:4]
    even_ref, odd_ref = refs[4:]
    results = []
    for parity in (0, 1):
        factor = mode_factor(act_ref.shape[2:], parity, lat_rows)
        mixed = [
            (dot(act_ref[parity, g], second_ref[g]) * factor).astype(BF) for g in range(2)
        ]
        results.append(to_cells(inv_ref[parity], *mixed))
    store_halves(lax.axis_index("lon"), outs, *results, even_ref, odd_ref)


def weight_terms(full, group):
    size = full.shape[0] // 2
    upper, lower = full[:size], swap_groups(full[size:])
    return choose(upper + lower, upper - lower if group == 0 else lower - upper)


def backward_kernel(lat_rows, *refs):
    slots = refs[:4]
    fwd_ref, second_ref, slope_ref, spec_t, act_t = refs[4:9]
    pre_ref, keep_ref, send_ref = refs[9:12]
    sums, diffs, grad_ref = refs[12:]
    load_halves(lax.axis_index("lon"), slots, sums, diffs)
    terms = [[0.0, 0.0], [0.0, 0.0]]
    for parity, half in ((0, sums), (1, diffs)):
        modes = to_modes(fwd_ref[parity], half)
        factor = mode_factor(modes[0].shape, parity, lat_rows)
        size = modes[0].shape[0]
        span = slice(parity * size, (parity + 1) * size)
        for group in range(2):
            dual = (modes[group] * factor).astype(BF)
            pre = (dot(dual, second_ref[group]) * slope_ref[parity, group]).astype(BF)
            pre_ref[parity, group] = pre
            terms[0][group] += dot(spec_t[group, :, span], pre)
            terms[1][group] += dot(act_t[group, :, span], dual)
    for tensor in range(2):
        both = [weight_terms(terms[tensor][group], group).astype(BF) for group in range(2)]
        grad_ref[tensor] = pack(jnp.concatenate(both, axis=0))
    side = lax.axis_index("dp") % 2
    keep_ref[...] = grad_ref[side]
    send_ref[...] = grad_ref[1 - side]


def return_kernel(pre_ref, inv_ref, first_ref, *refs):
    outs = refs[:4]
    even_ref, odd_ref = refs[4:]
    results = []
    for parity in (0, 1):
        spec = [dot(pre_ref[parity, g], first_ref[g]).astype(BF) for g in range(2)]
        results.append(to_cells(inv_ref[parity], *spec))
    store_halves(lax.axis_index("lon"), outs, *results, even_ref, odd_ref)


def spread_kernel(scale, places, *refs):
    count = len(places)
    pieces, outs, held, sems = refs[:count], refs[-4:-2], refs[-2], refs[-1]
    me, side = lax.axis_index("lon"), lax.axis_index("dp") % 2
    width = held.shape[-1]

    def each_copy(index, act):
        mask, other = places[index]
        for tensor in range(2):

            @pl.when((side ^ other) == tensor)
            def _():
                act(
                    pltpu.make_async_copy(
                        held.at[index],
                        outs[tensor].at[:, pl.ds(2 * (me ^ mask), 2)],
                        sems.at[index],
                    )
                )

    for index in range(count):
        rows = unpack(pieces[index][...]).astype(F32) * scale
        for group in range(2):
            block = rows[group * width : (group + 1) * width]
            held[index, 0, group] = block[:, :width]
            held[index, 1, group] = block[:, width:]
        each_copy(index, lambda copy: copy.start())
    for index in range(count):
        each_copy(index, lambda copy: copy.wait())


VMEM = pl.BlockSpec(memory_space=pltpu.VMEM)
HBM = pl.BlockSpec(memory_space=pltpu.HBM)


def call(kernel, outs, args, scratch=(), in_hbm=(), out_hbm=False, aliases=None, vmem_mib=20):
    return pl.pallas_call(
        kernel,
        out_shape=outs,
        in_specs=[HBM if i in in_hbm or i in (aliases or {}) else VMEM for i in range(len(args))],
        out_specs=[HBM if out_hbm else VMEM] * len(outs),
        scratch_shapes=scratch,
        input_output_aliases=aliases or {},
        compiler_params=pltpu.CompilerParams(vmem_limit_bytes=vmem_mib * 2**20),
        cost_estimate=pl.CostEstimate(flops=1, bytes_accessed=1, transcendentals=0),
    )(*args)


def swap(value, axis, mask):
    size = lax.axis_size(axis)
    return lax.ppermute(value, axis, [(i, i ^ mask) for i in range(size)])


def flip_pairs(dp_count, lon_count, dp_mask, lon_mask):
    return [
        (d * lon_count + i, (d ^ dp_mask) * lon_count + (i ^ lon_mask))
        for d in range(dp_count)
        for i in range(lon_count)
    ]


def after(*values):
    return lax.optimization_barrier(values)


def added(left, right):
    return (left.astype(F32) + right.astype(F32)).astype(BF)


def by_groups(fields, cotangent, first_weight, second_weight):
    _, cells, lat_rows, channels = fields.shape
    groups, group_width = first_weight.shape[1], first_weight.shape[2]
    lon_count = lax.axis_size("lon")
    sample_count = lax.axis_size("dp")
    width = groups // lon_count * group_width
    total_cells = cells * lon_count
    rows = cells * lat_rows
    half = 2 * rows
    forward, inverse = (jnp.asarray(t) for t in dft_tables(total_cells, lat_rows))
    packed = jax.ShapeDtypeStruct((rows * width // 128, 128), BF)
    piece = jax.ShapeDtypeStruct((4 * group_width * width // 256, 128), BF)

    def trade(slots):
        across, corner, beside = (swap(slots[m], "lon", m) for m in (2, 3, 1))
        return [slots[0], beside, across, corner]

    def own(weight):
        return lax.dynamic_slice_in_dim(weight, lax.axis_index("lon") * 2, 2, axis=1)

    halves = [pltpu.VMEM((2, 2, rows, width), BF)] * 2
    results = [pltpu.VMEM((2, rows, width), F32)] * 2

    field_slots = trade(call(pack_kernel, [packed] * 4, [fields]))
    cot_slots = trade(call(pack_kernel, [packed] * 4, [cotangent]))
    matrix = jax.ShapeDtypeStruct((2, width, width), BF)
    table = jax.ShapeDtypeStruct(forward.shape, BF)
    first_mat, first_adj, second_mat, second_adj, forward = call(
        weight_kernel,
        [matrix] * 4 + [table],
        [own(first_weight), own(second_weight), forward],
        [pltpu.SemaphoreType.DMA((2,))],
        in_hbm=(2,),
        vmem_mib=48,
    )
    modes_shape = jax.ShapeDtypeStruct((2, 2, rows, width), BF)
    slope_shape = jax.ShapeDtypeStruct((2, 2, rows, width), F32)
    turned_shape = jax.ShapeDtypeStruct((2, width, half), BF)
    act, slope, spec_t, act_t = call(
        inner_kernel,
        [modes_shape, slope_shape, turned_shape, turned_shape],
        [*field_slots, forward, first_mat],
        halves,
    )
    wave = call(
        functools.partial(wave_kernel, lat_rows), [packed] * 4, [act, inverse, second_mat], results
    )
    wave_slots = trade(wave)
    cot_slots, wave = after(cot_slots, wave)
    pre, keep, send = call(
        functools.partial(backward_kernel, lat_rows),
        [modes_shape, piece, piece],
        [*cot_slots, forward, second_adj, slope, spec_t, act_t],
        halves + [pltpu.VMEM((2, *piece.shape), BF)],
    )
    other = swap(send, "dp", 1)
    pull = call(return_kernel, [packed] * 4, [pre, inverse, first_adj], results)
    other, pull, wave_slots = after(other, pull, wave_slots)
    pull_slots = trade(pull)
    grad = added(keep, other)
    grid_shape = jax.ShapeDtypeStruct(fields.shape, BF)
    (layer_out,) = call(merge_kernel, [grid_shape], [fields, *wave_slots])
    mask = 2
    while mask < sample_count:
        other = swap(grad, "dp", mask)
        if mask == 4:
            other, layer_out, pull_slots[1:3] = after(other, layer_out, pull_slots[1:3])
        grad = added(grad, other)
        mask *= 2
    beside = swap(grad, "lon", 1)
    (field_grad,) = call(merge_kernel, [grid_shape], [cotangent, *pull_slots])
    across, flipped, corner = (
        lax.ppermute(grad, ("dp", "lon"), flip_pairs(sample_count, lon_count, d, i))
        for d, i in ((0, 2), (1, 0), (1, 2))
    )
    beside, corner, field_grad = after(beside, corner, field_grad)
    grad_shape = jax.ShapeDtypeStruct(first_weight.shape, F32)

    def spread(places, pieces, outs=()):
        return call(
            functools.partial(spread_kernel, 1.0 / sample_count, places),
            [grad_shape] * 2,
            [*pieces, *outs],
            [
                pltpu.VMEM((len(places), 2, 2, group_width, group_width), F32),
                pltpu.SemaphoreType.DMA((len(places),)),
            ],
            out_hbm=True,
            aliases={len(pieces) + i: i for i in range(len(outs))},
        )

    corner_core = swap(corner, "lon", 1)
    early = spread(((2, 1), (0, 0), (1, 0)), [corner, grad, beside])
    across, *early = after(across, *early)
    across_core, flipped_core = swap(across, "lon", 1), swap(flipped, "lon", 1)
    first_grad, second_grad = spread(
        ((3, 1), (2, 0), (0, 1), (3, 0), (1, 1)),
        [corner_core, across, flipped, across_core, flipped_core],
        early,
    )
    return layer_out, field_grad, first_grad, second_grad


def owns_groups(mesh, fields, first_weight):
    lon_count, sample_count = mesh.shape["lon"], mesh.shape["dp"]
    _, cells, lat_rows, _ = fields.shape
    return (
        lon_count == 4
        and sample_count > 1
        and sample_count & (sample_count - 1) == 0
        and fields.shape[0] == sample_count
        and first_weight.shape[1:] == (8, 96, 96)
        and lat_rows % 16 == 0
        and cells % 8 == 0
    )


def solution(mesh):
    placed = (P("dp", "lon", None, None), P("dp", "lon", None, None), P(), P())

    def run(fields, cotangent, first_weight, second_weight):
        body = by_groups if owns_groups(mesh, fields, first_weight) else on_device
        return jax.shard_map(
            body, mesh=mesh, in_specs=placed, out_specs=placed, check_vma=False
        )(fields, cotangent, first_weight, second_weight)

    return run
```

```python
import functools
import math

import jax
import jax.numpy as jnp
import ml_dtypes
import numpy as np
from jax import lax
from jax.experimental import pallas as pl
from jax.experimental.pallas import tpu as pltpu
from jax.sharding import PartitionSpec as P

COEF = 0.7978845608028654
CUBIC = 0.044715


def gelu_value(inner):
    hyper = jnp.tanh(COEF * (inner + CUBIC * inner * inner * inner))
    return 0.5 * inner * (1.0 + hyper)


def gelu_slope(inner):
    hyper = jnp.tanh(COEF * (inner + CUBIC * inner * inner * inner))
    return 0.5 * (1.0 + hyper) + 0.5 * inner * (1.0 - hyper * hyper) * COEF * (
        1.0 + 3.0 * CUBIC * inner * inner
    )


def make_basis(length, count):
    cell_idx = jnp.arange(length, dtype=jnp.int32)
    mode_idx = jnp.arange(count, dtype=jnp.int32)
    product = cell_idx[:, None] * mode_idx[None, :] % length
    angle = product.astype(jnp.float32) * jnp.float32(2.0 * math.pi / length)
    return jnp.stack([jnp.cos(angle), -jnp.sin(angle)], axis=-1).astype(jnp.bfloat16)


def lat_apply(spec, table, lat_scale):
    return (
        jnp.einsum("kphc,phqj->kqjc", spec, table, preferred_element_type=jnp.float32) * lat_scale
    ).astype(jnp.bfloat16)


def forward_weight(weight):
    return jnp.stack([jnp.stack([weight[0], weight[1]]), jnp.stack([-weight[1], weight[0]])])


def adjoint_weight(weight):
    return jnp.stack([jnp.stack([weight[0], -weight[1]]), jnp.stack([weight[1], weight[0]])])


def block_product(spec, stacked):
    return jnp.einsum("kphbi,pqbij->kqhbj", spec, stacked, preferred_element_type=jnp.float32)


def block_adjoint(spec, stacked):
    return jnp.einsum("kphbj,pqbij->kqhbi", spec, stacked, preferred_element_type=jnp.float32)


def block_outer(left, right):
    pairs = jnp.einsum("kphbi,kqhbj->pqbij", left, right, preferred_element_type=jnp.float32)
    return jnp.stack([pairs[0, 0] + pairs[1, 1], pairs[0, 1] - pairs[1, 0]])


def on_device(fields, cotangent, first_weight, second_weight):
    cell_rows = fields[0]
    cot_rows = cotangent[0]
    lat_rows = cell_rows.shape[1]
    channels = cell_rows.shape[2]
    groups = first_weight.shape[1]
    group_width = first_weight.shape[2]
    lon_count = lax.axis_size("lon")
    total_cells = cell_rows.shape[0] * lon_count
    dft_basis = make_basis(total_cells, total_cells // 2)
    lat_basis = make_basis(lat_rows, lat_rows)
    cos_tab = lat_basis[:, :, 0]
    sin_tab = lat_basis[:, :, 1]
    lat_fwd_table = jnp.stack(
        [jnp.stack([cos_tab, sin_tab], axis=1), jnp.stack([-sin_tab, cos_tab], axis=1)], axis=0
    )
    lat_inv_table = jnp.stack(
        [jnp.stack([cos_tab.T, -sin_tab.T], axis=1), jnp.stack([sin_tab.T, cos_tab.T], axis=1)],
        axis=0,
    )
    norm_scale = 1.0 / math.sqrt(total_cells)
    lat_scale = 1.0 / math.sqrt(lat_rows)
    local_modes = cell_rows.shape[0] // 2
    mode_idx = lax.axis_index("lon") * local_modes + jnp.arange(local_modes, dtype=jnp.int32)
    mode_weight = jnp.where(mode_idx == 0, 1.0, 2.0).astype(jnp.bfloat16)[:, None, None, None]
    first_fwd = forward_weight(first_weight)
    second_fwd = forward_weight(second_weight)
    first_adj = adjoint_weight(first_weight)
    second_adj = adjoint_weight(second_weight)

    def local_dft(all_lines):
        return (
            jnp.einsum("whc,wkp->kphc", all_lines, dft_basis, preferred_element_type=jnp.float32)
            * norm_scale
        ).astype(jnp.bfloat16)

    def local_idft(all_modes):
        return (
            jnp.einsum("kphc,wkp->whc", all_modes, dft_basis, preferred_element_type=jnp.float32)
            * norm_scale
        ).astype(jnp.bfloat16)

    def lines_to_modes(all_lines):
        return lax.all_to_all(local_dft(all_lines), "lon", split_axis=0, concat_axis=3, tiled=True)

    def modes_to_lines(all_modes):
        return lax.all_to_all(local_idft(all_modes), "lon", split_axis=0, concat_axis=2, tiled=True)

    def to_spectrum(grid_rows):
        return lines_to_modes(
            lax.all_to_all(grid_rows, "lon", split_axis=2, concat_axis=0, tiled=True)
        )

    def to_cells(spec_rows):
        return modes_to_lines(
            lax.all_to_all(spec_rows, "lon", split_axis=3, concat_axis=0, tiled=True)
        )

    def split_groups(spec_rows):
        return spec_rows.reshape(local_modes, 2, lat_rows, groups, group_width)

    def join_groups(spec_rows):
        return spec_rows.astype(jnp.bfloat16).reshape(local_modes, 2, lat_rows, channels)

    lon_spec = to_spectrum(cell_rows)
    spectrum = split_groups(lat_apply(lon_spec, lat_fwd_table, lat_scale))
    inner = block_product(spectrum, first_fwd)
    act = gelu_value(inner).astype(jnp.bfloat16)
    mixed = join_groups(block_product(act, second_fwd)) * mode_weight
    mixed_lon = lat_apply(mixed, lat_inv_table, lat_scale)
    wave = to_cells(mixed_lon)
    dual_lon = to_spectrum(cot_rows)
    dual = split_groups(lat_apply(dual_lon, lat_fwd_table, lat_scale) * mode_weight)
    back = block_adjoint(dual, second_adj)
    pre = (back * gelu_slope(inner)).astype(jnp.bfloat16)
    back_spec = join_groups(block_adjoint(pre, first_adj))
    back_lon = lat_apply(back_spec, lat_inv_table, lat_scale)
    pull = to_cells(back_lon)
    layer_out = (cell_rows.astype(jnp.float32) + wave.astype(jnp.float32)).astype(jnp.bfloat16)
    field_grad = (cot_rows.astype(jnp.float32) + pull.astype(jnp.float32)).astype(jnp.bfloat16)
    sample_count = lax.axis_size("dp")
    second_term = block_outer(act, dual) / sample_count
    first_term = block_outer(spectrum, pre) / sample_count
    first_grad, second_grad = lax.psum((first_term, second_term), ("dp", "lon"))
    return (layer_out[None], field_grad[None], first_grad, second_grad)


BF = jnp.bfloat16
F32 = jnp.float32


def dft_tables(cells, lat_rows):
    half = cells // 2

    def basis(length, count):
        product = np.arange(length)[:, None] * np.arange(count)[None, :] % length
        angle = product.astype(np.float32) * np.float32(2.0 * math.pi / length)
        pair = np.stack([np.cos(angle), -np.sin(angle)], axis=-1).astype(np.float32)
        return pair.astype(ml_dtypes.bfloat16).astype(np.float64)

    lon = basis(cells, half)[:half]
    lat = basis(lat_rows, lat_rows)
    scale = 1.0 / math.sqrt(cells * lat_rows)
    real = np.einsum("wk,hj->kjwh", lon[..., 0], lat[..., 0]) - np.einsum(
        "wk,hj->kjwh", lon[..., 1], lat[..., 1]
    )
    imag = np.einsum("wk,hj->kjwh", lon[..., 1], lat[..., 0]) + np.einsum(
        "wk,hj->kjwh", lon[..., 0], lat[..., 1]
    )
    both = np.stack([real, imag]) * scale
    size = half * lat_rows
    tables = [both[:, p::2].reshape(size, size).astype(ml_dtypes.bfloat16) for p in (0, 1)]
    forward = np.stack(tables)
    inverse = np.stack([t.T for t in tables])
    return forward, np.ascontiguousarray(inverse)


def dot(left, right):
    return jnp.dot(left, right, preferred_element_type=F32)


def swap_groups(value):
    width = value.shape[-1] // 2
    return jnp.concatenate([value[:, width:], value[:, :width]], axis=1)


def choose(first, second):
    lane = lax.broadcasted_iota(jnp.int32, first.shape, 1)
    return jnp.where(lane < first.shape[1] // 2, first, second)


def pack(rows):
    half = rows.shape[0] // 2
    tail = rows[:, 128:]
    return jnp.concatenate(
        [rows[:, :128], jnp.concatenate([tail[:half], tail[half:]], axis=1)], axis=0
    )


def unpack(packed):
    count = packed.shape[0] * 2 // 3
    tail = packed[count:]
    return jnp.concatenate(
        [packed[:count], jnp.concatenate([tail[:, :64], tail[:, 64:]], axis=0)], axis=1
    )


def pack_kernel(grid_ref, *outs):
    me = lax.axis_index("lon")
    _, cells, lat_rows, channels = grid_ref.shape
    width = channels // 4
    for here in range(4):

        @pl.when(me == here)
        def _():
            rows = grid_ref[...].reshape(cells * lat_rows, channels)
            for slot in range(4):
                there = here ^ slot
                outs[slot][...] = pack(rows[:, there * width : (there + 1) * width])


def weight_kernel(first_ref, second_ref, table_hbm, *refs):
    outs, table_ref, sems = refs[:4], refs[4], refs[5]
    tables = [
        pltpu.make_async_copy(table_hbm.at[p], table_ref.at[p], sems.at[p]) for p in range(2)
    ]
    for copy in tables:
        copy.start()
    for i, weight_ref in enumerate((first_ref, second_ref)):
        for group in range(2):
            real, imag = weight_ref[0, group], weight_ref[1, group]
            cross = imag if group == 0 else -imag
            matrix = jnp.concatenate(
                [
                    jnp.concatenate([real, cross], axis=1),
                    jnp.concatenate([-cross, real], axis=1),
                ],
                axis=0,
            )
            outs[2 * i][group] = matrix
            outs[2 * i + 1][group] = matrix.T
    for copy in tables:
        copy.wait()


def merge_kernel(grid_ref, *refs):
    slots, out_ref = refs[:4], refs[4]
    me = lax.axis_index("lon")
    _, cells, lat_rows, channels = grid_ref.shape
    for here in range(4):

        @pl.when(me == here)
        def _():
            rows = jnp.concatenate([unpack(slots[here ^ s][...]) for s in range(4)], axis=1)
            total = grid_ref[...].astype(F32) + rows.astype(F32).reshape(grid_ref.shape)
            out_ref[...] = total.astype(BF)


def load_halves(me, slots, sums, diffs):
    core = me % 2
    sign = jnp.where(me < 2, 1.0, -1.0).astype(F32)
    for slot, spot in ((0, core), (1, 1 - core)):
        near = slots[slot][...].astype(F32)
        far = slots[slot + 2][...].astype(F32)
        for both, packed in ((sums, near + far), (diffs, sign * (near - far))):
            both[spot] = unpack(packed.astype(BF))


def to_modes(table, cells, factor):
    size = table.shape[0] // 2
    rows = cells[...].reshape(-1, cells.shape[-1])
    real = (dot(table[:size], rows) * factor).astype(BF)
    imag = swap_groups((dot(table[size:], rows) * factor).astype(BF))
    return choose(real, imag), choose(imag, real)


def to_cells(table, first, second):
    return dot(table, jnp.concatenate([choose(first, second), swap_groups(choose(second, first))], axis=0))


def store_halves(me, outs, even, odd, even_ref, odd_ref):
    core = me % 2
    sign = jnp.where(me < 2, 1.0, -1.0).astype(F32)
    even_ref[...] = even.reshape(even_ref.shape)
    odd_ref[...] = odd.reshape(odd_ref.shape)
    for slot, spot in ((0, core), (1, 1 - core)):
        near = even_ref[spot]
        far = sign * odd_ref[spot]
        outs[slot][...] = pack((near + far).astype(BF))
        outs[slot + 2][...] = pack((near - far).astype(BF))


def mode_factor(shape, parity, lat_rows):
    if parity == 1:
        return 2.0
    row = lax.broadcasted_iota(jnp.int32, shape, 0)
    return jnp.where(row < lat_rows, 1.0, 2.0).astype(F32)


def gelu_both(u):
    square = u * u
    hyper = jnp.tanh(COEF * (u + CUBIC * square * u))
    value = 0.5 * u * (1.0 + hyper)
    slope = 0.5 * (1.0 + hyper) + 0.5 * u * (1.0 - hyper * hyper) * COEF * (
        1.0 + 3.0 * CUBIC * square
    )
    return value, slope


def inner_kernel(*refs):
    slots = refs[:4]
    fwd_ref, first_ref = refs[4:6]
    act_ref, slope_ref, spec_t, act_t = refs[6:10]
    sums, diffs = refs[10:]
    load_halves(lax.axis_index("lon"), slots, sums, diffs)
    for parity, half in ((0, sums), (1, diffs)):
        modes = to_modes(fwd_ref[parity], half, 1.0)
        for group in range(2):
            spec = modes[group]
            act, slope = gelu_both(dot(spec, first_ref[group]))
            act = act.astype(BF)
            size = act.shape[0]
            act_ref[parity, group] = act
            slope_ref[parity, group] = slope
            spec_t[group, :, parity * size : (parity + 1) * size] = spec.T
            act_t[group, :, parity * size : (parity + 1) * size] = act.T


def wave_kernel(lat_rows, act_ref, inv_ref, second_ref, *refs):
    outs = refs[:4]
    even_ref, odd_ref = refs[4:]
    results = []
    for parity in (0, 1):
        factor = mode_factor(act_ref.shape[2:], parity, lat_rows)
        mixed = [
            (dot(act_ref[parity, g], second_ref[g]) * factor).astype(BF) for g in range(2)
        ]
        results.append(to_cells(inv_ref[parity], *mixed))
    store_halves(lax.axis_index("lon"), outs, *results, even_ref, odd_ref)


def weight_terms(full, group):
    size = full.shape[0] // 2
    upper, lower = full[:size], swap_groups(full[size:])
    return choose(upper + lower, upper - lower if group == 0 else lower - upper)


def backward_kernel(lat_rows, *refs):
    slots = refs[:4]
    fwd_ref, second_ref, slope_ref, spec_t, act_t = refs[4:9]
    pre_ref, keep_ref, send_ref = refs[9:12]
    sums, diffs, grad_ref = refs[12:]
    load_halves(lax.axis_index("lon"), slots, sums, diffs)
    terms = [[0.0, 0.0], [0.0, 0.0]]
    for parity, half in ((0, sums), (1, diffs)):
        size = fwd_ref.shape[1] // 2
        factor = mode_factor((size, half.shape[-1]), parity, lat_rows)
        modes = to_modes(fwd_ref[parity], half, factor)
        span = slice(parity * size, (parity + 1) * size)
        for group in range(2):
            dual = modes[group]
            pre = (dot(dual, second_ref[group]) * slope_ref[parity, group]).astype(BF)
            pre_ref[parity, group] = pre
            terms[0][group] += dot(spec_t[group, :, span], pre)
            terms[1][group] += dot(act_t[group, :, span], dual)
    for tensor in range(2):
        both = [weight_terms(terms[tensor][group], group).astype(BF) for group in range(2)]
        grad_ref[tensor] = pack(jnp.concatenate(both, axis=0))
    side = lax.axis_index("dp") % 2
    keep_ref[...] = grad_ref[side]
    send_ref[...] = grad_ref[1 - side]


def return_kernel(pre_ref, inv_ref, first_ref, *refs):
    outs = refs[:4]
    even_ref, odd_ref = refs[4:]
    results = []
    for parity in (0, 1):
        spec = [dot(pre_ref[parity, g], first_ref[g]).astype(BF) for g in range(2)]
        results.append(to_cells(inv_ref[parity], *spec))
    store_halves(lax.axis_index("lon"), outs, *results, even_ref, odd_ref)


def spread_kernel(scale, places, *refs):
    count = len(places)
    pieces, outs, held, sems = refs[:count], refs[-4:-2], refs[-2], refs[-1]
    me, side = lax.axis_index("lon"), lax.axis_index("dp") % 2
    width = held.shape[-1]

    def each_copy(index, act):
        mask, other = places[index]
        for tensor in range(2):

            @pl.when((side ^ other) == tensor)
            def _():
                act(
                    pltpu.make_async_copy(
                        held.at[index],
                        outs[tensor].at[:, pl.ds(2 * (me ^ mask), 2)],
                        sems.at[index],
                    )
                )

    for index in range(count):
        rows = unpack(pieces[index][...]).astype(F32) * scale
        for group in range(2):
            block = rows[group * width : (group + 1) * width]
            held[index, 0, group] = block[:, :width]
            held[index, 1, group] = block[:, width:]
        each_copy(index, lambda copy: copy.start())
    for index in range(count):
        each_copy(index, lambda copy: copy.wait())


VMEM = pl.BlockSpec(memory_space=pltpu.VMEM)
HBM = pl.BlockSpec(memory_space=pltpu.HBM)


def call(kernel, outs, args, scratch=(), in_hbm=(), out_hbm=False, aliases=None, vmem_mib=20):
    return pl.pallas_call(
        kernel,
        out_shape=outs,
        in_specs=[HBM if i in in_hbm or i in (aliases or {}) else VMEM for i in range(len(args))],
        out_specs=[HBM if out_hbm else VMEM] * len(outs),
        scratch_shapes=scratch,
        input_output_aliases=aliases or {},
        compiler_params=pltpu.CompilerParams(vmem_limit_bytes=vmem_mib * 2**20),
        cost_estimate=pl.CostEstimate(flops=1, bytes_accessed=1, transcendentals=0),
    )(*args)


def swap(value, axis, mask):
    size = lax.axis_size(axis)
    return lax.ppermute(value, axis, [(i, i ^ mask) for i in range(size)])


def flip_pairs(dp_count, lon_count, dp_mask, lon_mask):
    return [
        (d * lon_count + i, (d ^ dp_mask) * lon_count + (i ^ lon_mask))
        for d in range(dp_count)
        for i in range(lon_count)
    ]


def after(*values):
    return lax.optimization_barrier(values)


def added(left, right):
    return (left.astype(F32) + right.astype(F32)).astype(BF)


def by_groups(fields, cotangent, first_weight, second_weight):
    _, cells, lat_rows, channels = fields.shape
    groups, group_width = first_weight.shape[1], first_weight.shape[2]
    lon_count = lax.axis_size("lon")
    sample_count = lax.axis_size("dp")
    width = groups // lon_count * group_width
    total_cells = cells * lon_count
    rows = cells * lat_rows
    half = 2 * rows
    forward, inverse = (jnp.asarray(t) for t in dft_tables(total_cells, lat_rows))
    packed = jax.ShapeDtypeStruct((rows * width // 128, 128), BF)
    piece = jax.ShapeDtypeStruct((4 * group_width * width // 256, 128), BF)

    def trade(slots):
        across, corner, beside = (swap(slots[m], "lon", m) for m in (2, 3, 1))
        return [slots[0], beside, across, corner]

    def own(weight):
        return lax.dynamic_slice_in_dim(weight, lax.axis_index("lon") * 2, 2, axis=1)

    halves = [pltpu.VMEM((2, rows, width), BF)] * 2
    results = [pltpu.VMEM((2, rows, width), F32)] * 2

    field_slots = trade(call(pack_kernel, [packed] * 4, [fields]))
    cot_slots = trade(call(pack_kernel, [packed] * 4, [cotangent]))
    matrix = jax.ShapeDtypeStruct((2, width, width), BF)
    table = jax.ShapeDtypeStruct(forward.shape, BF)
    first_mat, first_adj, second_mat, second_adj, forward = call(
        weight_kernel,
        [matrix] * 4 + [table],
        [own(first_weight), own(second_weight), forward],
        [pltpu.SemaphoreType.DMA((2,))],
        in_hbm=(2,),
        vmem_mib=48,
    )
    modes_shape = jax.ShapeDtypeStruct((2, 2, rows, width), BF)
    slope_shape = jax.ShapeDtypeStruct((2, 2, rows, width), F32)
    turned_shape = jax.ShapeDtypeStruct((2, width, half), BF)
    act, slope, spec_t, act_t = call(
        inner_kernel,
        [modes_shape, slope_shape, turned_shape, turned_shape],
        [*field_slots, forward, first_mat],
        halves,
    )
    wave = call(
        functools.partial(wave_kernel, lat_rows), [packed] * 4, [act, inverse, second_mat], results
    )
    wave_slots = trade(wave)
    cot_slots, wave = after(cot_slots, wave)
    pre, keep, send = call(
        functools.partial(backward_kernel, lat_rows),
        [modes_shape, piece, piece],
        [*cot_slots, forward, second_adj, slope, spec_t, act_t],
        halves + [pltpu.VMEM((2, *piece.shape), BF)],
    )
    other = swap(send, "dp", 1)
    pull = call(return_kernel, [packed] * 4, [pre, inverse, first_adj], results)
    other, pull, wave_slots = after(other, pull, wave_slots)
    pull_slots = trade(pull)
    grad = added(keep, other)
    grid_shape = jax.ShapeDtypeStruct(fields.shape, BF)
    (layer_out,) = call(merge_kernel, [grid_shape], [fields, *wave_slots])
    mask = 2
    while mask < sample_count:
        other = swap(grad, "dp", mask)
        if mask == 4:
            other, layer_out, pull_slots[2] = after(other, layer_out, pull_slots[2])
        grad = added(grad, other)
        mask *= 2
    beside = swap(grad, "lon", 1)
    (field_grad,) = call(merge_kernel, [grid_shape], [cotangent, *pull_slots])
    across, flipped, corner = (
        lax.ppermute(grad, ("dp", "lon"), flip_pairs(sample_count, lon_count, d, i))
        for d, i in ((0, 2), (1, 0), (1, 2))
    )
    beside, corner, field_grad = after(beside, corner, field_grad)
    grad_shape = jax.ShapeDtypeStruct(first_weight.shape, F32)

    def spread(places, pieces, outs=()):
        return call(
            functools.partial(spread_kernel, 1.0 / sample_count, places),
            [grad_shape] * 2,
            [*pieces, *outs],
            [
                pltpu.VMEM((len(places), 2, 2, group_width, group_width), F32),
                pltpu.SemaphoreType.DMA((len(places),)),
            ],
            out_hbm=True,
            aliases={len(pieces) + i: i for i in range(len(outs))},
        )

    corner_core = swap(corner, "lon", 1)
    early = spread(((2, 1), (0, 0), (1, 0)), [corner, grad, beside])
    across, *early = after(across, *early)
    across_core, flipped_core = swap(across, "lon", 1), swap(flipped, "lon", 1)
    early = spread(((2, 0), (3, 1)), [across, corner_core], early)
    first_grad, second_grad = spread(
        ((0, 1), (3, 0), (1, 1)), [flipped, across_core, flipped_core], early
    )
    return layer_out, field_grad, first_grad, second_grad


def owns_groups(mesh, fields, first_weight):
    lon_count, sample_count = mesh.shape["lon"], mesh.shape["dp"]
    _, cells, lat_rows, _ = fields.shape
    return (
        lon_count == 4
        and sample_count > 1
        and sample_count & (sample_count - 1) == 0
        and fields.shape[0] == sample_count
        and first_weight.shape[1:] == (8, 96, 96)
        and lat_rows % 16 == 0
        and cells % 8 == 0
    )


def solution(mesh):
    placed = (P("dp", "lon", None, None), P("dp", "lon", None, None), P(), P())

    def run(fields, cotangent, first_weight, second_weight):
        body = by_groups if owns_groups(mesh, fields, first_weight) else on_device
        return jax.shard_map(
            body, mesh=mesh, in_specs=placed, out_specs=placed, check_vma=False
        )(fields, cotangent, first_weight, second_weight)

    return run
```

```python
import functools
import math

import jax
import jax.numpy as jnp
import ml_dtypes
import numpy as np
from jax import lax
from jax.experimental import pallas as pl
from jax.experimental.pallas import tpu as pltpu
from jax.sharding import PartitionSpec as P

COEF = 0.7978845608028654
CUBIC = 0.044715


def gelu_value(inner):
    hyper = jnp.tanh(COEF * (inner + CUBIC * inner * inner * inner))
    return 0.5 * inner * (1.0 + hyper)


def gelu_slope(inner):
    hyper = jnp.tanh(COEF * (inner + CUBIC * inner * inner * inner))
    return 0.5 * (1.0 + hyper) + 0.5 * inner * (1.0 - hyper * hyper) * COEF * (
        1.0 + 3.0 * CUBIC * inner * inner
    )


def make_basis(length, count):
    cell_idx = jnp.arange(length, dtype=jnp.int32)
    mode_idx = jnp.arange(count, dtype=jnp.int32)
    product = cell_idx[:, None] * mode_idx[None, :] % length
    angle = product.astype(jnp.float32) * jnp.float32(2.0 * math.pi / length)
    return jnp.stack([jnp.cos(angle), -jnp.sin(angle)], axis=-1).astype(jnp.bfloat16)


def lat_apply(spec, table, lat_scale):
    return (
        jnp.einsum("kphc,phqj->kqjc", spec, table, preferred_element_type=jnp.float32) * lat_scale
    ).astype(jnp.bfloat16)


def forward_weight(weight):
    return jnp.stack([jnp.stack([weight[0], weight[1]]), jnp.stack([-weight[1], weight[0]])])


def adjoint_weight(weight):
    return jnp.stack([jnp.stack([weight[0], -weight[1]]), jnp.stack([weight[1], weight[0]])])


def block_product(spec, stacked):
    return jnp.einsum("kphbi,pqbij->kqhbj", spec, stacked, preferred_element_type=jnp.float32)


def block_adjoint(spec, stacked):
    return jnp.einsum("kphbj,pqbij->kqhbi", spec, stacked, preferred_element_type=jnp.float32)


def block_outer(left, right):
    pairs = jnp.einsum("kphbi,kqhbj->pqbij", left, right, preferred_element_type=jnp.float32)
    return jnp.stack([pairs[0, 0] + pairs[1, 1], pairs[0, 1] - pairs[1, 0]])


def on_device(fields, cotangent, first_weight, second_weight):
    cell_rows = fields[0]
    cot_rows = cotangent[0]
    lat_rows = cell_rows.shape[1]
    channels = cell_rows.shape[2]
    groups = first_weight.shape[1]
    group_width = first_weight.shape[2]
    lon_count = lax.axis_size("lon")
    total_cells = cell_rows.shape[0] * lon_count
    dft_basis = make_basis(total_cells, total_cells // 2)
    lat_basis = make_basis(lat_rows, lat_rows)
    cos_tab = lat_basis[:, :, 0]
    sin_tab = lat_basis[:, :, 1]
    lat_fwd_table = jnp.stack(
        [jnp.stack([cos_tab, sin_tab], axis=1), jnp.stack([-sin_tab, cos_tab], axis=1)], axis=0
    )
    lat_inv_table = jnp.stack(
        [jnp.stack([cos_tab.T, -sin_tab.T], axis=1), jnp.stack([sin_tab.T, cos_tab.T], axis=1)],
        axis=0,
    )
    norm_scale = 1.0 / math.sqrt(total_cells)
    lat_scale = 1.0 / math.sqrt(lat_rows)
    local_modes = cell_rows.shape[0] // 2
    mode_idx = lax.axis_index("lon") * local_modes + jnp.arange(local_modes, dtype=jnp.int32)
    mode_weight = jnp.where(mode_idx == 0, 1.0, 2.0).astype(jnp.bfloat16)[:, None, None, None]
    first_fwd = forward_weight(first_weight)
    second_fwd = forward_weight(second_weight)
    first_adj = adjoint_weight(first_weight)
    second_adj = adjoint_weight(second_weight)

    def local_dft(all_lines):
        return (
            jnp.einsum("whc,wkp->kphc", all_lines, dft_basis, preferred_element_type=jnp.float32)
            * norm_scale
        ).astype(jnp.bfloat16)

    def local_idft(all_modes):
        return (
            jnp.einsum("kphc,wkp->whc", all_modes, dft_basis, preferred_element_type=jnp.float32)
            * norm_scale
        ).astype(jnp.bfloat16)

    def lines_to_modes(all_lines):
        return lax.all_to_all(local_dft(all_lines), "lon", split_axis=0, concat_axis=3, tiled=True)

    def modes_to_lines(all_modes):
        return lax.all_to_all(local_idft(all_modes), "lon", split_axis=0, concat_axis=2, tiled=True)

    def to_spectrum(grid_rows):
        return lines_to_modes(
            lax.all_to_all(grid_rows, "lon", split_axis=2, concat_axis=0, tiled=True)
        )

    def to_cells(spec_rows):
        return modes_to_lines(
            lax.all_to_all(spec_rows, "lon", split_axis=3, concat_axis=0, tiled=True)
        )

    def split_groups(spec_rows):
        return spec_rows.reshape(local_modes, 2, lat_rows, groups, group_width)

    def join_groups(spec_rows):
        return spec_rows.astype(jnp.bfloat16).reshape(local_modes, 2, lat_rows, channels)

    lon_spec = to_spectrum(cell_rows)
    spectrum = split_groups(lat_apply(lon_spec, lat_fwd_table, lat_scale))
    inner = block_product(spectrum, first_fwd)
    act = gelu_value(inner).astype(jnp.bfloat16)
    mixed = join_groups(block_product(act, second_fwd)) * mode_weight
    mixed_lon = lat_apply(mixed, lat_inv_table, lat_scale)
    wave = to_cells(mixed_lon)
    dual_lon = to_spectrum(cot_rows)
    dual = split_groups(lat_apply(dual_lon, lat_fwd_table, lat_scale) * mode_weight)
    back = block_adjoint(dual, second_adj)
    pre = (back * gelu_slope(inner)).astype(jnp.bfloat16)
    back_spec = join_groups(block_adjoint(pre, first_adj))
    back_lon = lat_apply(back_spec, lat_inv_table, lat_scale)
    pull = to_cells(back_lon)
    layer_out = (cell_rows.astype(jnp.float32) + wave.astype(jnp.float32)).astype(jnp.bfloat16)
    field_grad = (cot_rows.astype(jnp.float32) + pull.astype(jnp.float32)).astype(jnp.bfloat16)
    sample_count = lax.axis_size("dp")
    second_term = block_outer(act, dual) / sample_count
    first_term = block_outer(spectrum, pre) / sample_count
    first_grad, second_grad = lax.psum((first_term, second_term), ("dp", "lon"))
    return (layer_out[None], field_grad[None], first_grad, second_grad)


BF = jnp.bfloat16
F32 = jnp.float32


def dft_tables(cells, lat_rows):
    half = cells // 2

    def basis(length, count):
        product = np.arange(length)[:, None] * np.arange(count)[None, :] % length
        angle = product.astype(np.float32) * np.float32(2.0 * math.pi / length)
        pair = np.stack([np.cos(angle), -np.sin(angle)], axis=-1).astype(np.float32)
        return pair.astype(ml_dtypes.bfloat16).astype(np.float64)

    lon = basis(cells, half)[:half]
    lat = basis(lat_rows, lat_rows)
    scale = 1.0 / math.sqrt(cells * lat_rows)
    real = np.einsum("wk,hj->kjwh", lon[..., 0], lat[..., 0]) - np.einsum(
        "wk,hj->kjwh", lon[..., 1], lat[..., 1]
    )
    imag = np.einsum("wk,hj->kjwh", lon[..., 1], lat[..., 0]) + np.einsum(
        "wk,hj->kjwh", lon[..., 0], lat[..., 1]
    )
    both = np.stack([real, imag]) * scale
    size = half * lat_rows
    tables = [both[:, p::2].reshape(size, size).astype(ml_dtypes.bfloat16) for p in (0, 1)]
    forward = np.stack(tables)
    inverse = np.stack([t.T for t in tables])
    return forward, np.ascontiguousarray(inverse)


def dot(left, right):
    return jnp.dot(left, right, preferred_element_type=F32)


def swap_groups(value):
    width = value.shape[-1] // 2
    return jnp.concatenate([value[:, width:], value[:, :width]], axis=1)


def choose(first, second):
    lane = lax.broadcasted_iota(jnp.int32, first.shape, 1)
    return jnp.where(lane < first.shape[1] // 2, first, second)


def pack(rows):
    half = rows.shape[0] // 2
    tail = rows[:, 128:]
    return jnp.concatenate(
        [rows[:, :128], jnp.concatenate([tail[:half], tail[half:]], axis=1)], axis=0
    )


def unpack(packed):
    count = packed.shape[0] * 2 // 3
    tail = packed[count:]
    return jnp.concatenate(
        [packed[:count], jnp.concatenate([tail[:, :64], tail[:, 64:]], axis=0)], axis=1
    )


def pack_kernel(grid_ref, *outs):
    me = lax.axis_index("lon")
    _, cells, lat_rows, channels = grid_ref.shape
    width = channels // 4
    for here in range(4):

        @pl.when(me == here)
        def _():
            rows = grid_ref[...].reshape(cells * lat_rows, channels)
            for slot in range(4):
                there = here ^ slot
                outs[slot][...] = pack(rows[:, there * width : (there + 1) * width])


def weight_kernel(first_ref, second_ref, table_hbm, *refs):
    outs, table_ref, sems = refs[:4], refs[4], refs[5]
    tables = [
        pltpu.make_async_copy(table_hbm.at[p], table_ref.at[p], sems.at[p]) for p in range(2)
    ]
    for copy in tables:
        copy.start()
    for i, weight_ref in enumerate((first_ref, second_ref)):
        for group in range(2):
            real, imag = weight_ref[0, group], weight_ref[1, group]
            cross = imag if group == 0 else -imag
            matrix = jnp.concatenate(
                [
                    jnp.concatenate([real, cross], axis=1),
                    jnp.concatenate([-cross, real], axis=1),
                ],
                axis=0,
            )
            outs[2 * i][group] = matrix
            outs[2 * i + 1][group] = matrix.T
    for copy in tables:
        copy.wait()


def merge_kernel(grid_ref, *refs):
    slots, out_ref = refs[:4], refs[4]
    me = lax.axis_index("lon")
    _, cells, lat_rows, channels = grid_ref.shape
    for here in range(4):

        @pl.when(me == here)
        def _():
            rows = jnp.concatenate([unpack(slots[here ^ s][...]) for s in range(4)], axis=1)
            total = grid_ref[...].astype(F32) + rows.astype(F32).reshape(grid_ref.shape)
            out_ref[...] = total.astype(BF)


def load_halves(me, slots, sums, diffs):
    core = me % 2
    sign = jnp.where(me < 2, 1.0, -1.0).astype(F32)
    for slot, spot in ((0, core), (1, 1 - core)):
        near = slots[slot][...].astype(F32)
        far = slots[slot + 2][...].astype(F32)
        for both, packed in ((sums, near + far), (diffs, sign * (near - far))):
            both[spot] = unpack(packed.astype(BF))


def to_modes(table, cells, factor):
    size = table.shape[0] // 2
    rows = cells[...].reshape(-1, cells.shape[-1])
    real = (dot(table[:size], rows) * factor).astype(BF)
    imag = swap_groups((dot(table[size:], rows) * factor).astype(BF))
    return choose(real, imag), choose(imag, real)


def to_cells(table, first, second):
    return dot(table, jnp.concatenate([choose(first, second), swap_groups(choose(second, first))], axis=0))


def store_halves(me, outs, even, odd, even_ref, odd_ref):
    core = me % 2
    sign = jnp.where(me < 2, 1.0, -1.0).astype(F32)
    even_ref[...] = even.reshape(even_ref.shape)
    odd_ref[...] = odd.reshape(odd_ref.shape)
    for slot, spot in ((0, core), (1, 1 - core)):
        near = even_ref[spot]
        far = sign * odd_ref[spot]
        outs[slot][...] = pack((near + far).astype(BF))
        outs[slot + 2][...] = pack((near - far).astype(BF))


def mode_factor(shape, parity, lat_rows):
    if parity == 1:
        return 2.0
    row = lax.broadcasted_iota(jnp.int32, shape, 0)
    return jnp.where(row < lat_rows, 1.0, 2.0).astype(F32)


def gelu_both(u):
    square = u * u
    hyper = jnp.tanh(COEF * (u + CUBIC * square * u))
    value = 0.5 * u * (1.0 + hyper)
    slope = 0.5 * (1.0 + hyper) + 0.5 * u * (1.0 - hyper * hyper) * COEF * (
        1.0 + 3.0 * CUBIC * square
    )
    return value, slope


def inner_kernel(*refs):
    slots = refs[:4]
    fwd_ref, first_ref = refs[4:6]
    act_ref, slope_ref, spec_t, act_t = refs[6:10]
    sums, diffs = refs[10:]
    load_halves(lax.axis_index("lon"), slots, sums, diffs)
    for parity, half in ((0, sums), (1, diffs)):
        modes = to_modes(fwd_ref[parity], half, 1.0)
        for group in range(2):
            spec = modes[group]
            act, slope = gelu_both(dot(spec, first_ref[group]))
            act = act.astype(BF)
            size = act.shape[0]
            act_ref[parity, group] = act
            slope_ref[parity, group] = slope
            spec_t[group, :, parity * size : (parity + 1) * size] = spec.T
            act_t[group, :, parity * size : (parity + 1) * size] = act.T


def wave_kernel(lat_rows, act_ref, inv_ref, second_ref, *refs):
    outs = refs[:4]
    even_ref, odd_ref = refs[4:]
    results = []
    for parity in (0, 1):
        factor = mode_factor(act_ref.shape[2:], parity, lat_rows)
        mixed = [
            (dot(act_ref[parity, g], second_ref[g]) * factor).astype(BF) for g in range(2)
        ]
        results.append(to_cells(inv_ref[parity], *mixed))
    store_halves(lax.axis_index("lon"), outs, *results, even_ref, odd_ref)


def weight_terms(full, group):
    size = full.shape[0] // 2
    upper, lower = full[:size], swap_groups(full[size:])
    return choose(upper + lower, upper - lower if group == 0 else lower - upper)


def backward_kernel(lat_rows, *refs):
    slots = refs[:4]
    fwd_ref, second_ref, slope_ref, spec_t, act_t = refs[4:9]
    pre_ref, keep_ref, send_ref = refs[9:12]
    sums, diffs, grad_ref = refs[12:]
    load_halves(lax.axis_index("lon"), slots, sums, diffs)
    terms = [[0.0, 0.0], [0.0, 0.0]]
    for parity, half in ((0, sums), (1, diffs)):
        size = fwd_ref.shape[1] // 2
        factor = mode_factor((size, half.shape[-1]), parity, lat_rows)
        modes = to_modes(fwd_ref[parity], half, factor)
        span = slice(parity * size, (parity + 1) * size)
        for group in range(2):
            dual = modes[group]
            pre = (dot(dual, second_ref[group]) * slope_ref[parity, group]).astype(BF)
            pre_ref[parity, group] = pre
            terms[0][group] += dot(spec_t[group, :, span], pre)
            terms[1][group] += dot(act_t[group, :, span], dual)
    for tensor in range(2):
        both = [weight_terms(terms[tensor][group], group).astype(BF) for group in range(2)]
        grad_ref[tensor] = pack(jnp.concatenate(both, axis=0))
    side = lax.axis_index("dp") % 2
    keep_ref[...] = grad_ref[side]
    send_ref[...] = grad_ref[1 - side]


def return_kernel(pre_ref, inv_ref, first_ref, *refs):
    outs = refs[:4]
    even_ref, odd_ref = refs[4:]
    results = []
    for parity in (0, 1):
        spec = [dot(pre_ref[parity, g], first_ref[g]).astype(BF) for g in range(2)]
        results.append(to_cells(inv_ref[parity], *spec))
    store_halves(lax.axis_index("lon"), outs, *results, even_ref, odd_ref)


def spread_kernel(scale, places, *refs):
    count = len(places)
    pieces, outs, held, sems = refs[:count], refs[-4:-2], refs[-2], refs[-1]
    me, side = lax.axis_index("lon"), lax.axis_index("dp") % 2
    width = held.shape[-1]

    def each_copy(index, act):
        mask, other = places[index]
        for tensor in range(2):

            @pl.when((side ^ other) == tensor)
            def _():
                act(
                    pltpu.make_async_copy(
                        held.at[index],
                        outs[tensor].at[:, pl.ds(2 * (me ^ mask), 2)],
                        sems.at[index],
                    )
                )

    for index in range(count):
        rows = unpack(pieces[index][...]).astype(F32) * scale
        for group in range(2):
            block = rows[group * width : (group + 1) * width]
            held[index, 0, group] = block[:, :width]
            held[index, 1, group] = block[:, width:]
        each_copy(index, lambda copy: copy.start())
    for index in range(count):
        each_copy(index, lambda copy: copy.wait())


VMEM = pl.BlockSpec(memory_space=pltpu.VMEM)
HBM = pl.BlockSpec(memory_space=pltpu.HBM)


def call(kernel, outs, args, scratch=(), in_hbm=(), out_hbm=False, aliases=None, vmem_mib=20):
    return pl.pallas_call(
        kernel,
        out_shape=outs,
        in_specs=[HBM if i in in_hbm or i in (aliases or {}) else VMEM for i in range(len(args))],
        out_specs=[HBM if out_hbm else VMEM] * len(outs),
        scratch_shapes=scratch,
        input_output_aliases=aliases or {},
        compiler_params=pltpu.CompilerParams(vmem_limit_bytes=vmem_mib * 2**20),
        cost_estimate=pl.CostEstimate(flops=1, bytes_accessed=1, transcendentals=0),
    )(*args)


def swap(value, axis, mask):
    size = lax.axis_size(axis)
    return lax.ppermute(value, axis, [(i, i ^ mask) for i in range(size)])


def flip_pairs(dp_count, lon_count, dp_mask, lon_mask):
    return [
        (d * lon_count + i, (d ^ dp_mask) * lon_count + (i ^ lon_mask))
        for d in range(dp_count)
        for i in range(lon_count)
    ]


def after(*values):
    return lax.optimization_barrier(values)


def added(left, right):
    return (left.astype(F32) + right.astype(F32)).astype(BF)


def by_groups(fields, cotangent, first_weight, second_weight):
    _, cells, lat_rows, channels = fields.shape
    groups, group_width = first_weight.shape[1], first_weight.shape[2]
    lon_count = lax.axis_size("lon")
    sample_count = lax.axis_size("dp")
    width = groups // lon_count * group_width
    total_cells = cells * lon_count
    rows = cells * lat_rows
    half = 2 * rows
    forward, inverse = (jnp.asarray(t) for t in dft_tables(total_cells, lat_rows))
    packed = jax.ShapeDtypeStruct((rows * width // 128, 128), BF)
    piece = jax.ShapeDtypeStruct((4 * group_width * width // 256, 128), BF)

    def trade(slots):
        across, corner, beside = (swap(slots[m], "lon", m) for m in (2, 3, 1))
        return [slots[0], beside, across, corner]

    def own(weight):
        return lax.dynamic_slice_in_dim(weight, lax.axis_index("lon") * 2, 2, axis=1)

    halves = [pltpu.VMEM((2, rows, width), BF)] * 2
    results = [pltpu.VMEM((2, rows, width), F32)] * 2

    field_slots = trade(call(pack_kernel, [packed] * 4, [fields]))
    cot_slots = trade(call(pack_kernel, [packed] * 4, [cotangent]))
    matrix = jax.ShapeDtypeStruct((2, width, width), BF)
    table = jax.ShapeDtypeStruct(forward.shape, BF)
    first_mat, first_adj, second_mat, second_adj, forward = call(
        weight_kernel,
        [matrix] * 4 + [table],
        [own(first_weight), own(second_weight), forward],
        [pltpu.SemaphoreType.DMA((2,))],
        in_hbm=(2,),
        vmem_mib=48,
    )
    modes_shape = jax.ShapeDtypeStruct((2, 2, rows, width), BF)
    slope_shape = jax.ShapeDtypeStruct((2, 2, rows, width), F32)
    turned_shape = jax.ShapeDtypeStruct((2, width, half), BF)
    act, slope, spec_t, act_t = call(
        inner_kernel,
        [modes_shape, slope_shape, turned_shape, turned_shape],
        [*field_slots, forward, first_mat],
        halves,
    )
    wave = call(
        functools.partial(wave_kernel, lat_rows), [packed] * 4, [act, inverse, second_mat], results
    )
    wave_slots = trade(wave)
    cot_slots, wave = after(cot_slots, wave)
    pre, keep, send = call(
        functools.partial(backward_kernel, lat_rows),
        [modes_shape, piece, piece],
        [*cot_slots, forward, second_adj, slope, spec_t, act_t],
        halves + [pltpu.VMEM((2, *piece.shape), BF)],
    )
    other = swap(send, "dp", 1)
    pull = call(return_kernel, [packed] * 4, [pre, inverse, first_adj], results)
    other, pull, wave_slots = after(other, pull, wave_slots)
    pull_slots = trade(pull)
    grad = added(keep, other)
    grid_shape = jax.ShapeDtypeStruct(fields.shape, BF)
    (layer_out,) = call(merge_kernel, [grid_shape], [fields, *wave_slots])
    mask = 2
    while mask < sample_count:
        other = swap(grad, "dp", mask)
        if mask == 4:
            other, layer_out, pull_slots[2] = after(other, layer_out, pull_slots[2])
        grad = added(grad, other)
        mask *= 2
    beside = swap(grad, "lon", 1)
    (field_grad,) = call(merge_kernel, [grid_shape], [cotangent, *pull_slots])
    across, flipped, corner = (
        lax.ppermute(grad, ("dp", "lon"), flip_pairs(sample_count, lon_count, d, i))
        for d, i in ((0, 2), (1, 0), (1, 2))
    )
    beside, corner, field_grad = after(beside, corner, field_grad)
    grad_shape = jax.ShapeDtypeStruct(first_weight.shape, F32)

    def spread(places, pieces, outs=()):
        return call(
            functools.partial(spread_kernel, 1.0 / sample_count, places),
            [grad_shape] * 2,
            [*pieces, *outs],
            [
                pltpu.VMEM((len(places), 2, 2, group_width, group_width), F32),
                pltpu.SemaphoreType.DMA((len(places),)),
            ],
            out_hbm=True,
            aliases={len(pieces) + i: i for i in range(len(outs))},
        )

    corner_core = swap(corner, "lon", 1)
    early = spread(((2, 1), (0, 0), (1, 0)), [corner, grad, beside])
    across, *early = after(across, *early)
    across_core, flipped_core = swap(across, "lon", 1), swap(flipped, "lon", 1)
    early = spread(((2, 0), (3, 1), (0, 1)), [across, corner_core, flipped], early)
    first_grad, second_grad = spread(
        ((3, 0), (1, 1)), [across_core, flipped_core], early
    )
    return layer_out, field_grad, first_grad, second_grad


def owns_groups(mesh, fields, first_weight):
    lon_count, sample_count = mesh.shape["lon"], mesh.shape["dp"]
    _, cells, lat_rows, _ = fields.shape
    return (
        lon_count == 4
        and sample_count > 1
        and sample_count & (sample_count - 1) == 0
        and fields.shape[0] == sample_count
        and first_weight.shape[1:] == (8, 96, 96)
        and lat_rows % 16 == 0
        and cells % 8 == 0
    )


def solution(mesh):
    placed = (P("dp", "lon", None, None), P("dp", "lon", None, None), P(), P())

    def run(fields, cotangent, first_weight, second_weight):
        body = by_groups if owns_groups(mesh, fields, first_weight) else on_device
        return jax.shard_map(
            body, mesh=mesh, in_specs=placed, out_specs=placed, check_vma=False
        )(fields, cotangent, first_weight, second_weight)

    return run
```

```python
import functools
import math

import jax
import jax.numpy as jnp
import ml_dtypes
import numpy as np
from jax import lax
from jax.experimental import pallas as pl
from jax.experimental.pallas import tpu as pltpu
from jax.sharding import PartitionSpec as P

COEF = 0.7978845608028654
CUBIC = 0.044715


def gelu_value(inner):
    hyper = jnp.tanh(COEF * (inner + CUBIC * inner * inner * inner))
    return 0.5 * inner * (1.0 + hyper)


def gelu_slope(inner):
    hyper = jnp.tanh(COEF * (inner + CUBIC * inner * inner * inner))
    return 0.5 * (1.0 + hyper) + 0.5 * inner * (1.0 - hyper * hyper) * COEF * (
        1.0 + 3.0 * CUBIC * inner * inner
    )


def make_basis(length, count):
    cell_idx = jnp.arange(length, dtype=jnp.int32)
    mode_idx = jnp.arange(count, dtype=jnp.int32)
    product = cell_idx[:, None] * mode_idx[None, :] % length
    angle = product.astype(jnp.float32) * jnp.float32(2.0 * math.pi / length)
    return jnp.stack([jnp.cos(angle), -jnp.sin(angle)], axis=-1).astype(jnp.bfloat16)


def lat_apply(spec, table, lat_scale):
    return (
        jnp.einsum("kphc,phqj->kqjc", spec, table, preferred_element_type=jnp.float32) * lat_scale
    ).astype(jnp.bfloat16)


def forward_weight(weight):
    return jnp.stack([jnp.stack([weight[0], weight[1]]), jnp.stack([-weight[1], weight[0]])])


def adjoint_weight(weight):
    return jnp.stack([jnp.stack([weight[0], -weight[1]]), jnp.stack([weight[1], weight[0]])])


def block_product(spec, stacked):
    return jnp.einsum("kphbi,pqbij->kqhbj", spec, stacked, preferred_element_type=jnp.float32)


def block_adjoint(spec, stacked):
    return jnp.einsum("kphbj,pqbij->kqhbi", spec, stacked, preferred_element_type=jnp.float32)


def block_outer(left, right):
    pairs = jnp.einsum("kphbi,kqhbj->pqbij", left, right, preferred_element_type=jnp.float32)
    return jnp.stack([pairs[0, 0] + pairs[1, 1], pairs[0, 1] - pairs[1, 0]])


def on_device(fields, cotangent, first_weight, second_weight):
    cell_rows = fields[0]
    cot_rows = cotangent[0]
    lat_rows = cell_rows.shape[1]
    channels = cell_rows.shape[2]
    groups = first_weight.shape[1]
    group_width = first_weight.shape[2]
    lon_count = lax.axis_size("lon")
    total_cells = cell_rows.shape[0] * lon_count
    dft_basis = make_basis(total_cells, total_cells // 2)
    lat_basis = make_basis(lat_rows, lat_rows)
    cos_tab = lat_basis[:, :, 0]
    sin_tab = lat_basis[:, :, 1]
    lat_fwd_table = jnp.stack(
        [jnp.stack([cos_tab, sin_tab], axis=1), jnp.stack([-sin_tab, cos_tab], axis=1)], axis=0
    )
    lat_inv_table = jnp.stack(
        [jnp.stack([cos_tab.T, -sin_tab.T], axis=1), jnp.stack([sin_tab.T, cos_tab.T], axis=1)],
        axis=0,
    )
    norm_scale = 1.0 / math.sqrt(total_cells)
    lat_scale = 1.0 / math.sqrt(lat_rows)
    local_modes = cell_rows.shape[0] // 2
    mode_idx = lax.axis_index("lon") * local_modes + jnp.arange(local_modes, dtype=jnp.int32)
    mode_weight = jnp.where(mode_idx == 0, 1.0, 2.0).astype(jnp.bfloat16)[:, None, None, None]
    first_fwd = forward_weight(first_weight)
    second_fwd = forward_weight(second_weight)
    first_adj = adjoint_weight(first_weight)
    second_adj = adjoint_weight(second_weight)

    def local_dft(all_lines):
        return (
            jnp.einsum("whc,wkp->kphc", all_lines, dft_basis, preferred_element_type=jnp.float32)
            * norm_scale
        ).astype(jnp.bfloat16)

    def local_idft(all_modes):
        return (
            jnp.einsum("kphc,wkp->whc", all_modes, dft_basis, preferred_element_type=jnp.float32)
            * norm_scale
        ).astype(jnp.bfloat16)

    def lines_to_modes(all_lines):
        return lax.all_to_all(local_dft(all_lines), "lon", split_axis=0, concat_axis=3, tiled=True)

    def modes_to_lines(all_modes):
        return lax.all_to_all(local_idft(all_modes), "lon", split_axis=0, concat_axis=2, tiled=True)

    def to_spectrum(grid_rows):
        return lines_to_modes(
            lax.all_to_all(grid_rows, "lon", split_axis=2, concat_axis=0, tiled=True)
        )

    def to_cells(spec_rows):
        return modes_to_lines(
            lax.all_to_all(spec_rows, "lon", split_axis=3, concat_axis=0, tiled=True)
        )

    def split_groups(spec_rows):
        return spec_rows.reshape(local_modes, 2, lat_rows, groups, group_width)

    def join_groups(spec_rows):
        return spec_rows.astype(jnp.bfloat16).reshape(local_modes, 2, lat_rows, channels)

    lon_spec = to_spectrum(cell_rows)
    spectrum = split_groups(lat_apply(lon_spec, lat_fwd_table, lat_scale))
    inner = block_product(spectrum, first_fwd)
    act = gelu_value(inner).astype(jnp.bfloat16)
    mixed = join_groups(block_product(act, second_fwd)) * mode_weight
    mixed_lon = lat_apply(mixed, lat_inv_table, lat_scale)
    wave = to_cells(mixed_lon)
    dual_lon = to_spectrum(cot_rows)
    dual = split_groups(lat_apply(dual_lon, lat_fwd_table, lat_scale) * mode_weight)
    back = block_adjoint(dual, second_adj)
    pre = (back * gelu_slope(inner)).astype(jnp.bfloat16)
    back_spec = join_groups(block_adjoint(pre, first_adj))
    back_lon = lat_apply(back_spec, lat_inv_table, lat_scale)
    pull = to_cells(back_lon)
    layer_out = (cell_rows.astype(jnp.float32) + wave.astype(jnp.float32)).astype(jnp.bfloat16)
    field_grad = (cot_rows.astype(jnp.float32) + pull.astype(jnp.float32)).astype(jnp.bfloat16)
    sample_count = lax.axis_size("dp")
    second_term = block_outer(act, dual) / sample_count
    first_term = block_outer(spectrum, pre) / sample_count
    first_grad, second_grad = lax.psum((first_term, second_term), ("dp", "lon"))
    return (layer_out[None], field_grad[None], first_grad, second_grad)


BF = jnp.bfloat16
F32 = jnp.float32


def dft_tables(cells, lat_rows):
    half = cells // 2

    def basis(length, count):
        product = np.arange(length)[:, None] * np.arange(count)[None, :] % length
        angle = product.astype(np.float32) * np.float32(2.0 * math.pi / length)
        pair = np.stack([np.cos(angle), -np.sin(angle)], axis=-1).astype(np.float32)
        return pair.astype(ml_dtypes.bfloat16).astype(np.float64)

    lon = basis(cells, half)[:half]
    lat = basis(lat_rows, lat_rows)
    scale = 1.0 / math.sqrt(cells * lat_rows)
    real = np.einsum("wk,hj->kjwh", lon[..., 0], lat[..., 0]) - np.einsum(
        "wk,hj->kjwh", lon[..., 1], lat[..., 1]
    )
    imag = np.einsum("wk,hj->kjwh", lon[..., 1], lat[..., 0]) + np.einsum(
        "wk,hj->kjwh", lon[..., 0], lat[..., 1]
    )
    both = np.stack([real, imag]) * scale
    size = half * lat_rows
    tables = [both[:, p::2].reshape(size, size).astype(ml_dtypes.bfloat16) for p in (0, 1)]
    forward = np.stack(tables)
    inverse = np.stack([t.T for t in tables])
    return forward, np.ascontiguousarray(inverse)


def dot(left, right):
    return jnp.dot(left, right, preferred_element_type=F32)


def swap_groups(value):
    width = value.shape[-1] // 2
    return jnp.concatenate([value[:, width:], value[:, :width]], axis=1)


def choose(first, second):
    lane = lax.broadcasted_iota(jnp.int32, first.shape, 1)
    return jnp.where(lane < first.shape[1] // 2, first, second)


def pack(rows):
    half = rows.shape[0] // 2
    tail = rows[:, 128:]
    return jnp.concatenate(
        [rows[:, :128], jnp.concatenate([tail[:half], tail[half:]], axis=1)], axis=0
    )


def unpack(packed):
    count = packed.shape[0] * 2 // 3
    tail = packed[count:]
    return jnp.concatenate(
        [packed[:count], jnp.concatenate([tail[:, :64], tail[:, 64:]], axis=0)], axis=1
    )


def pack_kernel(grid_ref, *outs):
    me = lax.axis_index("lon")
    _, cells, lat_rows, channels = grid_ref.shape
    width = channels // 4
    for here in range(4):

        @pl.when(me == here)
        def _():
            rows = grid_ref[...].reshape(cells * lat_rows, channels)
            for slot in range(4):
                there = here ^ slot
                outs[slot][...] = pack(rows[:, there * width : (there + 1) * width])


def weight_kernel(first_ref, second_ref, table_hbm, *refs):
    outs, table_ref, sems = refs[:4], refs[4], refs[5]
    tables = [
        pltpu.make_async_copy(table_hbm.at[p], table_ref.at[p], sems.at[p]) for p in range(2)
    ]
    for copy in tables:
        copy.start()
    for i, weight_ref in enumerate((first_ref, second_ref)):
        for group in range(2):
            real, imag = weight_ref[0, group], weight_ref[1, group]
            cross = imag if group == 0 else -imag
            matrix = jnp.concatenate(
                [
                    jnp.concatenate([real, cross], axis=1),
                    jnp.concatenate([-cross, real], axis=1),
                ],
                axis=0,
            )
            outs[2 * i][group] = matrix
            outs[2 * i + 1][group] = matrix.T
    for copy in tables:
        copy.wait()


def merge_kernel(grid_ref, *refs):
    slots, out_ref = refs[:4], refs[4]
    me = lax.axis_index("lon")
    _, cells, lat_rows, channels = grid_ref.shape
    for here in range(4):

        @pl.when(me == here)
        def _():
            rows = jnp.concatenate([unpack(slots[here ^ s][...]) for s in range(4)], axis=1)
            total = grid_ref[...].astype(F32) + rows.astype(F32).reshape(grid_ref.shape)
            out_ref[...] = total.astype(BF)


def load_halves(me, slots, sums, diffs):
    core = me % 2
    sign = jnp.where(me < 2, 1.0, -1.0).astype(F32)
    for slot, spot in ((0, core), (1, 1 - core)):
        near = slots[slot][...].astype(F32)
        far = slots[slot + 2][...].astype(F32)
        for both, packed in ((sums, near + far), (diffs, sign * (near - far))):
            both[spot] = unpack(packed.astype(BF))


def to_modes(table, cells, factor):
    size = table.shape[0] // 2
    rows = cells[...].reshape(-1, cells.shape[-1])
    real = (dot(table[:size], rows) * factor).astype(BF)
    imag = swap_groups((dot(table[size:], rows) * factor).astype(BF))
    return choose(real, imag), choose(imag, real)


def to_cells(table, first, second):
    return dot(table, jnp.concatenate([choose(first, second), swap_groups(choose(second, first))], axis=0))


def store_halves(me, outs, even, odd, even_ref, odd_ref):
    core = me % 2
    sign = jnp.where(me < 2, 1.0, -1.0).astype(F32)
    even_ref[...] = even.reshape(even_ref.shape)
    odd_ref[...] = odd.reshape(odd_ref.shape)
    for slot, spot in ((0, core), (1, 1 - core)):
        near = even_ref[spot]
        far = sign * odd_ref[spot]
        outs[slot][...] = pack((near + far).astype(BF))
        outs[slot + 2][...] = pack((near - far).astype(BF))


def mode_factor(shape, parity, lat_rows):
    if parity == 1:
        return 2.0
    row = lax.broadcasted_iota(jnp.int32, shape, 0)
    return jnp.where(row < lat_rows, 1.0, 2.0).astype(F32)


def gelu_both(u):
    square = u * u
    hyper = jnp.tanh(COEF * (u + CUBIC * square * u))
    value = 0.5 * u * (1.0 + hyper)
    slope = 0.5 * (1.0 + hyper) + 0.5 * u * (1.0 - hyper * hyper) * COEF * (
        1.0 + 3.0 * CUBIC * square
    )
    return value, slope


def inner_kernel(*refs):
    slots = refs[:4]
    fwd_ref, first_ref = refs[4:6]
    act_ref, slope_ref, spec_t, act_t = refs[6:10]
    sums, diffs = refs[10:]
    load_halves(lax.axis_index("lon"), slots, sums, diffs)
    for parity, half in ((0, sums), (1, diffs)):
        modes = to_modes(fwd_ref[parity], half, 1.0)
        for group in range(2):
            spec = modes[group]
            act, slope = gelu_both(dot(spec, first_ref[group]))
            act = act.astype(BF)
            size = act.shape[0]
            act_ref[parity, group] = act
            slope_ref[parity, group] = slope.astype(BF)
            spec_t[group, :, parity * size : (parity + 1) * size] = spec.T
            act_t[group, :, parity * size : (parity + 1) * size] = act.T


def wave_kernel(lat_rows, act_ref, inv_ref, second_ref, *refs):
    outs = refs[:4]
    even_ref, odd_ref = refs[4:]
    results = []
    for parity in (0, 1):
        factor = mode_factor(act_ref.shape[2:], parity, lat_rows)
        mixed = [
            (dot(act_ref[parity, g], second_ref[g]) * factor).astype(BF) for g in range(2)
        ]
        results.append(to_cells(inv_ref[parity], *mixed))
    store_halves(lax.axis_index("lon"), outs, *results, even_ref, odd_ref)


def weight_terms(full, group):
    size = full.shape[0] // 2
    upper, lower = full[:size], swap_groups(full[size:])
    return choose(upper + lower, upper - lower if group == 0 else lower - upper)


def backward_kernel(lat_rows, *refs):
    slots = refs[:4]
    fwd_ref, second_ref, slope_ref, spec_t, act_t = refs[4:9]
    pre_ref, keep_ref, send_ref = refs[9:12]
    sums, diffs, grad_ref = refs[12:]
    load_halves(lax.axis_index("lon"), slots, sums, diffs)
    terms = [[0.0, 0.0], [0.0, 0.0]]
    for parity, half in ((0, sums), (1, diffs)):
        size = fwd_ref.shape[1] // 2
        factor = mode_factor((size, half.shape[-1]), parity, lat_rows)
        modes = to_modes(fwd_ref[parity], half, factor)
        span = slice(parity * size, (parity + 1) * size)
        for group in range(2):
            dual = modes[group]
            pre = (dot(dual, second_ref[group]) * slope_ref[parity, group].astype(F32)).astype(BF)
            pre_ref[parity, group] = pre
            terms[0][group] += dot(spec_t[group, :, span], pre)
            terms[1][group] += dot(act_t[group, :, span], dual)
    for tensor in range(2):
        both = [weight_terms(terms[tensor][group], group).astype(BF) for group in range(2)]
        grad_ref[tensor] = pack(jnp.concatenate(both, axis=0))
    side = lax.axis_index("dp") % 2
    keep_ref[...] = grad_ref[side]
    send_ref[...] = grad_ref[1 - side]


def return_kernel(pre_ref, inv_ref, first_ref, *refs):
    outs = refs[:4]
    even_ref, odd_ref = refs[4:]
    results = []
    for parity in (0, 1):
        spec = [dot(pre_ref[parity, g], first_ref[g]).astype(BF) for g in range(2)]
        results.append(to_cells(inv_ref[parity], *spec))
    store_halves(lax.axis_index("lon"), outs, *results, even_ref, odd_ref)


def spread_kernel(scale, places, *refs):
    count = len(places)
    pieces, outs, held, sems = refs[:count], refs[-4:-2], refs[-2], refs[-1]
    me, side = lax.axis_index("lon"), lax.axis_index("dp") % 2
    width = held.shape[-1]

    def each_copy(index, act):
        mask, other = places[index]
        for tensor in range(2):

            @pl.when((side ^ other) == tensor)
            def _():
                act(
                    pltpu.make_async_copy(
                        held.at[index],
                        outs[tensor].at[:, pl.ds(2 * (me ^ mask), 2)],
                        sems.at[index],
                    )
                )

    for index in range(count):
        rows = unpack(pieces[index][...]).astype(F32) * scale
        for group in range(2):
            block = rows[group * width : (group + 1) * width]
            held[index, 0, group] = block[:, :width]
            held[index, 1, group] = block[:, width:]
        each_copy(index, lambda copy: copy.start())
    for index in range(count):
        each_copy(index, lambda copy: copy.wait())


VMEM = pl.BlockSpec(memory_space=pltpu.VMEM)
HBM = pl.BlockSpec(memory_space=pltpu.HBM)


def call(kernel, outs, args, scratch=(), in_hbm=(), out_hbm=False, aliases=None, vmem_mib=20):
    return pl.pallas_call(
        kernel,
        out_shape=outs,
        in_specs=[HBM if i in in_hbm or i in (aliases or {}) else VMEM for i in range(len(args))],
        out_specs=[HBM if out_hbm else VMEM] * len(outs),
        scratch_shapes=scratch,
        input_output_aliases=aliases or {},
        compiler_params=pltpu.CompilerParams(vmem_limit_bytes=vmem_mib * 2**20),
        cost_estimate=pl.CostEstimate(flops=1, bytes_accessed=1, transcendentals=0),
    )(*args)


def swap(value, axis, mask):
    size = lax.axis_size(axis)
    return lax.ppermute(value, axis, [(i, i ^ mask) for i in range(size)])


def flip_pairs(dp_count, lon_count, dp_mask, lon_mask):
    return [
        (d * lon_count + i, (d ^ dp_mask) * lon_count + (i ^ lon_mask))
        for d in range(dp_count)
        for i in range(lon_count)
    ]


def after(*values):
    return lax.optimization_barrier(values)


def added(left, right):
    return (left.astype(F32) + right.astype(F32)).astype(BF)


def by_groups(fields, cotangent, first_weight, second_weight):
    _, cells, lat_rows, channels = fields.shape
    groups, group_width = first_weight.shape[1], first_weight.shape[2]
    lon_count = lax.axis_size("lon")
    sample_count = lax.axis_size("dp")
    width = groups // lon_count * group_width
    total_cells = cells * lon_count
    rows = cells * lat_rows
    half = 2 * rows
    forward, inverse = (jnp.asarray(t) for t in dft_tables(total_cells, lat_rows))
    packed = jax.ShapeDtypeStruct((rows * width // 128, 128), BF)
    piece = jax.ShapeDtypeStruct((4 * group_width * width // 256, 128), BF)

    def trade(slots):
        across, corner, beside = (swap(slots[m], "lon", m) for m in (2, 3, 1))
        return [slots[0], beside, across, corner]

    def own(weight):
        return lax.dynamic_slice_in_dim(weight, lax.axis_index("lon") * 2, 2, axis=1)

    halves = [pltpu.VMEM((2, rows, width), BF)] * 2
    results = [pltpu.VMEM((2, rows, width), F32)] * 2

    field_slots = trade(call(pack_kernel, [packed] * 4, [fields]))
    cot_slots = trade(call(pack_kernel, [packed] * 4, [cotangent]))
    matrix = jax.ShapeDtypeStruct((2, width, width), BF)
    table = jax.ShapeDtypeStruct(forward.shape, BF)
    first_mat, first_adj, second_mat, second_adj, forward = call(
        weight_kernel,
        [matrix] * 4 + [table],
        [own(first_weight), own(second_weight), forward],
        [pltpu.SemaphoreType.DMA((2,))],
        in_hbm=(2,),
        vmem_mib=48,
    )
    modes_shape = jax.ShapeDtypeStruct((2, 2, rows, width), BF)
    slope_shape = jax.ShapeDtypeStruct((2, 2, rows, width), BF)
    turned_shape = jax.ShapeDtypeStruct((2, width, half), BF)
    act, slope, spec_t, act_t = call(
        inner_kernel,
        [modes_shape, slope_shape, turned_shape, turned_shape],
        [*field_slots, forward, first_mat],
        halves,
    )
    wave = call(
        functools.partial(wave_kernel, lat_rows), [packed] * 4, [act, inverse, second_mat], results
    )
    wave_slots = trade(wave)
    cot_slots, wave = after(cot_slots, wave)
    pre, keep, send = call(
        functools.partial(backward_kernel, lat_rows),
        [modes_shape, piece, piece],
        [*cot_slots, forward, second_adj, slope, spec_t, act_t],
        halves + [pltpu.VMEM((2, *piece.shape), BF)],
    )
    other = swap(send, "dp", 1)
    pull = call(return_kernel, [packed] * 4, [pre, inverse, first_adj], results)
    other, pull, wave_slots = after(other, pull, wave_slots)
    pull_slots = trade(pull)
    grad = added(keep, other)
    grid_shape = jax.ShapeDtypeStruct(fields.shape, BF)
    (layer_out,) = call(merge_kernel, [grid_shape], [fields, *wave_slots])
    mask = 2
    while mask < sample_count:
        other = swap(grad, "dp", mask)
        if mask == 4:
            other, layer_out, pull_slots[2] = after(other, layer_out, pull_slots[2])
        grad = added(grad, other)
        mask *= 2
    beside = swap(grad, "lon", 1)
    (field_grad,) = call(merge_kernel, [grid_shape], [cotangent, *pull_slots])
    across, flipped, corner = (
        lax.ppermute(grad, ("dp", "lon"), flip_pairs(sample_count, lon_count, d, i))
        for d, i in ((0, 2), (1, 0), (1, 2))
    )
    beside, corner, field_grad = after(beside, corner, field_grad)
    grad_shape = jax.ShapeDtypeStruct(first_weight.shape, F32)

    def spread(places, pieces, outs=()):
        return call(
            functools.partial(spread_kernel, 1.0 / sample_count, places),
            [grad_shape] * 2,
            [*pieces, *outs],
            [
                pltpu.VMEM((len(places), 2, 2, group_width, group_width), F32),
                pltpu.SemaphoreType.DMA((len(places),)),
            ],
            out_hbm=True,
            aliases={len(pieces) + i: i for i in range(len(outs))},
        )

    corner_core = swap(corner, "lon", 1)
    early = spread(((2, 1), (0, 0), (1, 0)), [corner, grad, beside])
    across, *early = after(across, *early)
    across_core, flipped_core = swap(across, "lon", 1), swap(flipped, "lon", 1)
    early = spread(((2, 0), (3, 1), (0, 1)), [across, corner_core, flipped], early)
    first_grad, second_grad = spread(
        ((3, 0), (1, 1)), [across_core, flipped_core], early
    )
    return layer_out, field_grad, first_grad, second_grad


def owns_groups(mesh, fields, first_weight):
    lon_count, sample_count = mesh.shape["lon"], mesh.shape["dp"]
    _, cells, lat_rows, _ = fields.shape
    return (
        lon_count == 4
        and sample_count > 1
        and sample_count & (sample_count - 1) == 0
        and fields.shape[0] == sample_count
        and first_weight.shape[1:] == (8, 96, 96)
        and lat_rows % 16 == 0
        and cells % 8 == 0
    )


def solution(mesh):
    placed = (P("dp", "lon", None, None), P("dp", "lon", None, None), P(), P())

    def run(fields, cotangent, first_weight, second_weight):
        body = by_groups if owns_groups(mesh, fields, first_weight) else on_device
        return jax.shard_map(
            body, mesh=mesh, in_specs=placed, out_specs=placed, check_vma=False
        )(fields, cotangent, first_weight, second_weight)

    return run
```
